256 devices in a mesh: outer: 32 (over x, y, core), inner: 8 (over z).
Axes of the slice: x: 4, y: 4, z: 8, core: 2. Of those that a mesh axis runs over, the one named last changes fastest.
Arguments:
- tokens: bfloat16 [65536, 2048], P(('outer', 'inner')), may hold values from -6 to 6
- norm_gain: float32 [2048], replicated, may hold values from 0.25 to 1.75
- norm_bias: float32 [2048], replicated, may hold values from -3 to 3
- keep_mask: int32 [65536, 2048], P(('outer', 'inner')), may hold values 0 or 1
- projection: bfloat16 [3, 2048, 2048], P(None, 'outer', 'inner'), may hold values from -0.125 to 0.125
- head_gain: float32 [2048], P('inner'), may hold values from 0.25 to 1.75
- traj_starts: int32 [8], replicated, may hold values from 0 to 65535, as said below
Outputs:
- attended: bfloat16 [65536, 2048], P('outer', 'inner')
The draws below stay inside these ranges and needn't reach their ends.
Inputs may be any that keep to these rules, and one draw needn't show every extreme that they name: `traj_starts`: 8 distinct positions in rising order, the first one 0 and the last one 65536 - 1; a trajectory runs from one entry to the next or to the row's end.
All inputs are finite; a program needn't handle non-finite values. No bound on the sum of `keep_mask` on one device may be relied on, other than what follows from the above.
Results may differ from the reference program's by a relative error of at most 0.0098.
Values may be sent and summed in bfloat16 or wider, within the bound.
A program may use at most 128 MiB of HBM per device.

```python
import jax
import jax.numpy as jnp
from jax import lax

D = 2048
HEADS = 16
HEAD_DIM = 128
SPAN = 512
NSEG = 8
TOKENS = 65536


def draw_traj_starts(key, part):
    key = jax.random.fold_in(key, 11)
    inner_starts = jax.random.choice(key, TOKENS - 2, (NSEG - 2,), replace=False) + 1
    ordered = jnp.sort(inner_starts.astype(jnp.int32))
    first = jnp.zeros((1,), jnp.int32)
    final = jnp.full((1,), TOKENS - 1, jnp.int32)
    return jnp.concatenate([first, ordered, final])


def set_ends(values, own_key, least, largest):
    extent = values.shape
    spot = [jax.random.randint(jax.random.fold_in(own_key, axis), (), 0, extent[axis]) for axis in range(len(extent))]
    values = values.at[tuple(spot)].set(least)
    longest = extent.index(max(extent))
    spot[longest] = (spot[longest] + 1) % extent[longest]
    return values.at[tuple(spot)].set(largest)


def block_levels(stream_key, extent, split, smallest, top_value):
    loudness, own = 1.0, jax.random.fold_in(stream_key, 6)
    for dim, blocks in split:
        draws = jnp.exp(jax.random.uniform(jax.random.fold_in(own, dim), (blocks,), jnp.float32, smallest / len(split), top_value / len(split)))
        loudness = loudness * jnp.repeat(draws, extent[dim] // blocks).reshape([-1 if axis == dim else 1 for axis in range(len(extent))])
    return loudness


def bell_draw(own_key, extent, width, bound, pieces=(), kind=jnp.bfloat16):
    result = jax.random.normal(own_key, extent, jnp.float32) * width
    if len(pieces) > 0:
        result = block_levels(own_key, extent, pieces, -0.22, 0.18) * result
    return jnp.clip(result, min=-bound, max=bound).astype(kind)


def setup_inputs(seed: int = 0) -> dict:
    streams_of = jax.random.split(jax.random.key(seed), 8)
    return {
        "tokens": bell_draw(streams_of[0], (TOKENS, D), 1.0, 6.0, ((0, 256),)),
        "norm_gain": jnp.clip(1.0 + 0.15 * jax.random.normal(streams_of[1], (D,), jnp.float32), 0.25, 1.75),
        "norm_bias": bell_draw(streams_of[2], (D,), 0.5, 3.0, (), jnp.float32),
        "keep_mask": set_ends((jax.random.randint(streams_of[3], (TOKENS, D), 0, 10) < 9).astype(jnp.int32), jax.random.fold_in(streams_of[3], 1), 0, 1),
        "projection": bell_draw(streams_of[4], (3, D, D), D ** -0.5, 0.125, ((1, 32), (2, 8))),
        "head_gain": jnp.clip(1.0 + 0.15 * jax.random.normal(streams_of[5], (D,), jnp.float32), 0.25, 1.75),
        "traj_starts": draw_traj_starts(jax.random.fold_in(streams_of[7], 71), 0),
    }


def segment_of(traj_starts, positions):
    hits = (traj_starts[None, :] <= positions[:, None]).astype(jnp.int32)
    return lax.optimization_barrier(jnp.sum(hits, axis=1)) - 1

def normalize(tokens, norm_gain, norm_bias, keep_mask):
    values = tokens.astype(jnp.float32)
    center = values - lax.optimization_barrier(jnp.mean(values, axis=-1, keepdims=True))
    spread = lax.optimization_barrier(jnp.mean(center * center, axis=-1, keepdims=True))
    scaled = (center * lax.rsqrt(spread + 1e-05) * norm_gain + norm_bias) * keep_mask.astype(jnp.float32) / 0.9
    return scaled.astype(jnp.bfloat16)

def span_step(carried, inputs_now):
    queries, keys_now, values_now, segment, before = inputs_now
    span_len = queries.shape[0]
    highest = lax.Precision.HIGHEST
    lower_mask = jnp.arange(span_len)[:, None] >= jnp.arange(span_len)[None, :]
    allowed = lower_mask & (segment[:, None] == segment[None, :])
    query_wide = queries.astype(jnp.float32)
    scores = jnp.einsum('thd,shd->hts', query_wide, keys_now.astype(jnp.float32), precision=highest)
    rounded = jnp.where(allowed[None], scores, 0.0).astype(jnp.bfloat16)
    inside_term = jnp.einsum('hts,shd->thd', rounded.astype(jnp.float32), values_now.astype(jnp.float32), precision=highest)
    reach_mask = (segment == before).astype(jnp.float32)
    carried_term = jnp.einsum('thd,hde->the', query_wide, carried, precision=highest)
    mixed = inside_term + carried_term * reach_mask[:, None, None]
    last_seg = segment[-1]
    kept_values = jnp.where((segment == last_seg)[:, None, None], values_now, jnp.zeros_like(values_now))
    update = jnp.einsum('shd,she->hde', keys_now.astype(jnp.float32), kept_values.astype(jnp.float32), precision=highest)
    carried = carried * (last_seg == before).astype(jnp.float32) + update
    return (carried, mixed)

def reference(tokens, norm_gain, norm_bias, keep_mask, projection, head_gain, traj_starts):
    span_count = TOKENS // SPAN
    positions = jnp.arange(TOKENS, dtype=jnp.int32)
    segment = segment_of(traj_starts, positions).reshape(span_count, SPAN)
    before = segment_of(traj_starts, jnp.arange(span_count, dtype=jnp.int32) * SPAN - 1)
    weights_wide = projection.astype(jnp.float32)

    def advance(carried, inputs_now):
        rows_now, mask_now, seg_now, before_now = inputs_now
        normed = normalize(rows_now, norm_gain, norm_bias, mask_now)
        projected = jnp.einsum('td,wdc->wtc', normed.astype(jnp.float32), weights_wide, precision=lax.Precision.HIGHEST).astype(jnp.bfloat16)
        queries = projected[0].reshape(SPAN, HEADS, HEAD_DIM)
        keys_now = projected[1].reshape(SPAN, HEADS, HEAD_DIM)
        values_now = projected[2].reshape(SPAN, HEADS, HEAD_DIM)
        carried, mixed = span_step(carried, (queries, keys_now, values_now, seg_now, before_now))
        scale_back = lax.rsqrt(lax.optimization_barrier(jnp.mean(mixed * mixed, axis=-1, keepdims=True)) + 1e-06)
        output = ((mixed * scale_back).reshape(SPAN, D) * head_gain).astype(jnp.bfloat16)
        return (carried, output)
    initial = jnp.zeros((HEADS, HEAD_DIM, HEAD_DIM), jnp.float32)
    inputs_all = (tokens.reshape(span_count, SPAN, D), keep_mask.reshape(span_count, SPAN, D), segment, before)
    unused, outputs = lax.scan(advance, initial, inputs_all)
    return outputs.reshape(TOKENS, D)
```

```python
import jax
import jax.numpy as jnp
from jax import lax
from jax.experimental import pallas as pl
from jax.experimental.pallas import tpu as pltpu
from jax.sharding import PartitionSpec as P

MESH = pl.DeviceIdType.MESH
F32, BF16, I32 = jnp.float32, jnp.bfloat16, jnp.int32
D, HEAD, SPAN = 2048, 128, 512
OWN = 256
PARTS = 4
PART = OWN // PARTS
RANGES = ((1, 2), (0, 1))
UNITS = ((0, 0), (1, 0), (0, 1), (1, 1))


def slot_of(dist):
    return 1 - dist // 2


def core_of(dist):
    return ((dist + 1) // 2) % 2


def plane_at(head_plane, dist):
    up = (head_plane + dist) % 8
    down = (head_plane + 8 - dist) % 8
    return jnp.where(up % 2 == 0, up, down)


def kernel(
    tok_hbm, gain, bias, mask_hbm, proj_hbm, head_gain, traj, out,
    tok, mask, x_all, w_all, qkv, inside, a_out, rz, local_c, t_all, tp, ps, p_all, c_out, cr, gains, outs,
    in_sem, wz_send, wz_recv, ring_send, ring_recv, tok_send, tok_recv, fwd_send, sib_recv, hg_send, hg_recv,
    rz_send, rz_recv, a2a_send, a2a_recv, cr_send, cr_recv, out_send, out_recv,
):
    outer, z = lax.axis_index("outer"), lax.axis_index("inner")
    core, chip = outer % 2, outer // 2
    cx, cy = chip // 4, chip % 4
    pair, member = z // 2, z % 2
    along = jnp.where(core == 0, cx, cy)
    across = jnp.where(core == 0, cy, cx)

    def chip_at(a, b):
        return a * (4 - 3 * core) + b * (1 + 3 * core)

    a_next, a_prev = (along + 1) % 4, (along + 3) % 4
    b_next, b_prev = (across + 1) % 4, (across + 3) % 4

    def plane_dev(chip_id):
        return (chip_id * 2 + core, z)

    def column_dev(core_id, plane):
        return (chip * 2 + core_id, plane)

    dists = (3 - core, core)
    step = 2 * member - 1
    planes = tuple((z + step * d + 8) % 8 for d in dists)

    def remote(src, dst, send, recv, device):
        return pltpu.make_async_remote_copy(
            src_ref=src, dst_ref=dst, send_sem=send, recv_sem=recv, device_id=device, device_id_type=MESH
        )

    def wait_for(ref, sem):
        pltpu.make_async_copy(ref, ref, sem).wait()

    def in_copies(i):
        rows = pl.ds(i * PART, PART)
        return (
            pltpu.make_async_copy(tok_hbm.at[rows], tok.at[rows], in_sem.at[0, i]),
            pltpu.make_async_copy(mask_hbm.at[rows], mask.at[rows], in_sem.at[1, i]),
        )

    for i in range(PARTS):
        for copy in in_copies(i):
            copy.start()

    barrier = pltpu.get_barrier_semaphore()

    def greet_plane(i, carry):
        pl.semaphore_signal(barrier, inc=1, device_id=plane_dev((chip + i) % 16), device_id_type=MESH)
        return carry

    def greet_column(i, carry):
        spot = (z * 2 + core + i) % 16
        pl.semaphore_signal(barrier, inc=1, device_id=column_dev(spot % 2, spot // 2), device_id_type=MESH)
        return carry

    lax.fori_loop(1, 16, greet_column, 0)
    lax.fori_loop(1, 16, greet_plane, 0)
    pl.semaphore_wait(barrier, 30)

    def wz_copy(d, r):
        first, count = RANGES[r]
        src = proj_hbm.at[pl.ds(first, count)]
        dst = w_all.at[slot_of(d), pl.ds(first, count), cx, cy, pl.ds(core * 64, 64)]
        return src, dst, wz_send.at[d, r], wz_recv.at[slot_of(d), r, core], column_dev(core_of(d), plane_at(z, d))

    for r in range(2):
        for d in (3, 2, 1, 0):
            src, dst, send, recv, device = wz_copy(d, r)
            if d == 0:

                @pl.when(core == 0)
                def _():
                    pltpu.make_async_copy(src, dst, recv).start()

                @pl.when(core == 1)
                def _():
                    remote(src, dst, send, recv, device).start()

            else:
                remote(src, dst, send, recv, device).start()
    for d in range(4):

        @pl.when((core == core_of(d)) if d else (core == 2))
        def _():
            s = slot_of(d)
            remote(head_gain, gains.at[s], hg_send.at[s], hg_recv.at[s], column_dev(core, plane_at(z, d))).start()

    @pl.when(core == 0)
    def _():
        gains[1] = head_gain[...]

    def wait_wz(u):
        s, r = UNITS[u]
        first, count = RANGES[r]
        for half in range(2):
            wait_for(w_all.at[s, pl.ds(first, count), 0, 0, pl.ds(half * 64, 64)], wz_recv.at[s, r, half])

    def block(u, chip_id, rows=None):
        s, r = UNITS[u]
        first, count = RANGES[r]
        ref = w_all.at[s, pl.ds(first, count), chip_id // 4, chip_id % 4]
        return ref if rows is None else ref.at[:, pl.ds(rows, 64)]

    def line_x(u, b, rows=None):
        s, r = UNITS[u]
        first, count = RANGES[r]
        ref = w_all.at[s, pl.ds(first, count), :, b]
        return ref if rows is None else ref.at[:, :, pl.ds(rows, 64)]

    def line_y(u, b, rows=None):
        s, r = UNITS[u]
        first, count = RANGES[r]
        ref = w_all.at[s, pl.ds(first, count), b]
        return ref if rows is None else ref.at[:, :, pl.ds(rows, 64)]

    def ring_sems(u, stage, way):
        return ring_send.at[u, stage, way], ring_recv.at[u, stage, way]

    a_devices = (plane_dev(chip_at(a_next, across)), plane_dev(chip_at(a_prev, across)))
    b_devices = (plane_dev(chip_at(along, b_next)), plane_dev(chip_at(along, b_prev)))

    def a1(u):
        wait_wz(u)
        for way in range(2):
            ref = block(u, chip)
            remote(ref, ref, *ring_sems(u, 0, way), a_devices[way]).start()

    def wait_ring(u, stage):
        for way in range(2):
            ref = line_y(u, 0, 64 * way if stage == 3 else None) if stage >= 2 else block(u, 0, 64 * way if stage == 1 else None)
            wait_for(ref, ring_recv.at[u, stage, way])

    def a2(u):
        wait_ring(u, 0)
        for way in range(2):
            ref = block(u, chip_at(a_prev if way == 0 else a_next, across), 64 * way)
            remote(ref, ref, *ring_sems(u, 1, way), a_devices[way]).start()

    def b_send(u, stage, spots, halves):
        @pl.when(core == 0)
        def _():
            for way in range(2):
                ref = line_x(u, spots[way], 64 * way if halves else None)
                remote(ref, ref, *ring_sems(u, stage, way), b_devices[way]).start()

        @pl.when(core == 1)
        def _():
            for way in range(2):
                ref = line_y(u, spots[way], 64 * way if halves else None)
                remote(ref, ref, *ring_sems(u, stage, way), b_devices[way]).start()

    def b1(u):
        wait_ring(u, 1)
        b_send(u, 2, (across, across), False)

    def b2(u):
        wait_ring(u, 2)
        b_send(u, 3, (b_prev, b_next), True)

    def b_done(u):
        wait_ring(u, 3)

    def ring_wait_sends(u):
        for stage in range(4):
            for way in range(2):
                half = 64 * way if stage in (1, 3) else None
                ref = line_y(u, 0, half) if stage >= 2 else block(u, 0, half)
                wait_for(ref, ring_send.at[u, stage, way])

    partner = column_dev(core, z + 1 - 2 * member)
    sibling = column_dev(1 - core, z)

    def token_rows(c, m, i):
        return x_all.at[c, m, pl.ds(i * PART, PART)]

    def normalize(i):
        for copy in in_copies(i):
            copy.wait()

        def rows16(j, carry):
            rows = pl.ds(pl.multiple_of(i * PART + j * 16, 16), 16)
            values = tok[rows, :].astype(F32)
            center = values - jnp.mean(values, axis=-1, keepdims=True)
            spread = jnp.mean(center * center, axis=-1, keepdims=True)
            scaled = center * lax.rsqrt(spread + 1e-05) * gain[...] + bias[...]
            x_all[core, member, rows, :] = (scaled * (mask[rows, :].astype(F32) * (1.0 / 0.9))).astype(BF16)
            return carry

        lax.fori_loop(0, PART // 16, rows16, 0)

    def send_tokens(i):
        ref = token_rows(core, member, i)
        remote(ref, ref, tok_send.at[0, i], tok_recv.at[i], partner).start()
        remote(ref, ref, tok_send.at[1, i], sib_recv.at[0, i], sibling).start()

    def forward_tokens(i):
        ref = token_rows(core, 1 - member, i)
        wait_for(ref, tok_recv.at[i])
        remote(ref, ref, fwd_send.at[i], sib_recv.at[1, i], sibling).start()

    def project(s, w, m):
        weights = w_all.at[s, w]

        def rows256(c, carry):
            product = jnp.dot(x_all[c, m], weights[...].reshape(D, 256), preferred_element_type=F32)
            rows = pl.ds(pl.multiple_of(m * OWN, OWN), OWN)
            qkv[s, w, c, rows, :] = product.astype(BF16)
            return carry

        lax.fori_loop(0, 2, rows256, 0)

    def start_of(position):
        first = jnp.full_like(position, -1)
        for i in range(8):
            first = jnp.where(traj[i] <= position, traj[i], first)
        return first

    def keeps(first, length):
        return jnp.where(start_of(first + (length - 1)) < first, 1.0, 0.0).astype(F32)

    chip_first = chip * 8 * SPAN

    def span_first(c):
        return chip_first + (c * 4 + pair) * SPAN

    def states(s):
        def one_span(c, carry):
            first = span_first(c)
            last_start = start_of(first + (SPAN - 1))
            spots = first + lax.broadcasted_iota(I32, (SPAN, HEAD), 0)
            kept = spots >= last_start
            for h in range(2):
                columns = slice(h * HEAD, (h + 1) * HEAD)
                values = jnp.where(kept, qkv[s, 2, c, :, columns].astype(F32), 0.0).astype(BF16)
                state = lax.dot_general(
                    qkv[s, 1, c, :, columns], values, (((0,), (0,)), ((), ())), preferred_element_type=F32
                )
                a_out[s, c, columns, :] = state.astype(BF16)
            return carry

        lax.fori_loop(0, 2, one_span, 0)

    def send_states(s):
        mine = dists[s]
        for i in range(1, 4):
            other = (mine + i) % 4
            remote(
                a_out.at[s, :, pl.ds(pl.multiple_of(other * 64, 64), 64)], rz.at[slot_of(other), :, pair],
                rz_send.at[s, i - 1], rz_recv.at[slot_of(other), pair],
                column_dev(core_of(other), plane_at(planes[s], other)),
            ).start()
        rz[s, :, pair] = a_out[s, :, pl.ds(pl.multiple_of(mine * 64, 64), 64), :]

    def wait_states(s):
        for i in range(1, 4):
            spot = (pair + i) % 4
            wait_for(rz.at[s, :, spot], rz_recv.at[s, spot])

    def chip_totals():
        for s in range(2):
            total = jnp.zeros((64, HEAD), F32)
            for j in range(8):
                local_c[j, s] = total
                total = total * keeps(chip_first + j * SPAN, SPAN) + rz[s, j // 4, j % 4].astype(F32)
            t_all[s * 64:(s + 1) * 64, :] = total

        def send(i, carry):
            other = (chip + i) % 16
            remote(
                t_all.at[pl.ds(pl.multiple_of(other * 8, 8), 8)], tp.at[chip], a2a_send.at[0], a2a_recv.at[0],
                plane_dev(other),
            ).start()
            return carry

        lax.fori_loop(1, 16, send, 0)
        tp[chip] = t_all[pl.ds(pl.multiple_of(chip * 8, 8), 8), :]

    def prefixes():
        wait_for(tp.at[pl.ds(0, 15)], a2a_recv.at[0])
        total = jnp.zeros((8, HEAD), F32)
        for k in range(16):
            ps[k] = total
            if k < 15:
                total = total * keeps(k * 8 * SPAN, 8 * SPAN) + tp[k]

        def send(i, carry):
            other = (chip + i) % 16
            remote(
                ps.at[other], p_all.at[pl.ds(pl.multiple_of(chip * 8, 8), 8)], a2a_send.at[1], a2a_recv.at[1],
                plane_dev(other),
            ).start()
            return carry

        lax.fori_loop(1, 16, send, 0)
        p_all[pl.ds(pl.multiple_of(chip * 8, 8), 8), :] = ps[chip]

    def carried():
        wait_for(tp.at[pl.ds(0, 15)], a2a_recv.at[1])
        reach = jnp.ones((), F32)
        for j in range(8):
            for s in range(2):
                total = local_c[j, s] + p_all[s * 64:(s + 1) * 64, :] * reach
                c_out[s, j // 4, j % 4] = total.astype(BF16)
            reach = reach * keeps(chip_first + j * SPAN, SPAN)
        for s in range(2):
            mine = dists[s]
            rows = pl.ds(pl.multiple_of(mine * 64, 64), 64)
            for i in range(1, 4):
                other = (mine + i) % 4
                plane = plane_at(planes[s], other)
                remote(
                    c_out.at[s, :, plane // 2], cr.at[slot_of(other), :, rows],
                    cr_send.at[s, i - 1], cr_recv.at[slot_of(other), mine],
                    column_dev(core_of(other), plane),
                ).start()
            cr[s, :, rows, :] = c_out[s, :, pair]

    def wait_carried(s):
        for i in range(1, 4):
            spot = (dists[s] + i) % 4
            wait_for(cr.at[s, :, pl.ds(0, 64)], cr_recv.at[s, spot])

    def inside_terms(s):
        def one_span(c, carry):
            first = span_first(c)
            for top in (0, 256):
                span_keys = top + 256
                rows = first + top + lax.broadcasted_iota(I32, (256, 1), 0)
                spots = first + lax.broadcasted_iota(I32, (256, span_keys), 1)
                allowed = (spots <= rows) & (spots >= start_of(rows))
                for h in range(2):
                    columns = slice(h * HEAD, (h + 1) * HEAD)
                    scores = lax.dot_general(
                        qkv[s, 0, c, top:top + 256, columns], qkv[s, 1, c, :span_keys, columns],
                        (((1,), (1,)), ((), ())), preferred_element_type=F32,
                    )
                    rounded = jnp.where(allowed, scores, 0.0).astype(BF16)
                    inside[s, c, top:top + 256, columns] = jnp.dot(
                        rounded, qkv[s, 2, c, :span_keys, columns], preferred_element_type=F32
                    )
            return carry

        lax.fori_loop(0, 2, one_span, 0)

    def finish(s):
        def one_span(c, carry):
            first = span_first(c)
            rows = first + lax.broadcasted_iota(I32, (SPAN, 1), 0)
            reached = start_of(rows) < first
            for h in range(2):
                columns = slice(h * HEAD, (h + 1) * HEAD)
                term = jnp.dot(qkv[s, 0, c, :, columns], cr[s, c, columns, :], preferred_element_type=F32)
                mixed = inside[s, c, :, columns] + jnp.where(reached, term, 0.0)
                scale_back = lax.rsqrt(jnp.mean(mixed * mixed, axis=-1, keepdims=True) + 1e-06)
                outs[s, c, :, columns] = (mixed * scale_back * gains[s, 0:1, columns]).astype(BF16)
            return carry

        lax.fori_loop(0, 2, one_span, 0)

    def send_out(s):
        rows = pl.ds(pl.multiple_of(pair * SPAN, SPAN), SPAN)
        for c in range(2):
            device = column_dev(c, planes[s])
            args = (outs.at[s, c], out.at[rows])
            if s == 1 and c == 0:

                @pl.when(core == 0)
                def _():
                    pltpu.make_async_copy(*args, out_recv.at[pair]).start()

                @pl.when(core == 1)
                def _():
                    remote(*args, out_send.at[s, c], out_recv.at[pair], device).start()

            else:
                remote(*args, out_send.at[s, c], out_recv.at[pair], device).start()

    normalize(0)
    send_tokens(0)
    a1(0)
    normalize(1)
    send_tokens(1)
    a1(1)
    normalize(2)
    send_tokens(2)
    a2(0)
    normalize(3)
    send_tokens(3)
    b1(0)
    a2(1)
    b1(1)
    a1(2)
    a1(3)
    forward_tokens(0)
    forward_tokens(1)
    b2(0)
    a2(2)
    a2(3)
    b_done(0)
    for i in range(PARTS):
        wait_for(token_rows(1 - core, member, i), sib_recv.at[0, i])
    for w in (1, 2):
        project(0, w, member)
    forward_tokens(2)
    b2(1)
    b1(2)
    forward_tokens(3)
    b1(3)
    b_done(1)
    for w in (1, 2):
        project(1, w, member)
    for i in range(PARTS):
        wait_for(token_rows(1 - core, 1 - member, i), sib_recv.at[1, i])
    for s in range(2):
        for w in (1, 2):
            project(s, w, 1 - member)
        states(s)
        send_states(s)
    b2(2)
    b_done(2)
    for s in range(2):
        wait_states(s)
    chip_totals()
    for m in range(2):
        project(0, 0, m)
    b2(3)
    prefixes()
    inside_terms(0)
    carried()
    b_done(3)
    for m in range(2):
        project(1, 0, m)
    inside_terms(1)
    wait_carried(0)

    @pl.when(core == 0)
    def _():
        wait_for(gains.at[0], hg_recv.at[0])

    @pl.when(core == 1)
    def _():
        for s in range(2):
            wait_for(gains.at[s], hg_recv.at[s])

    finish(0)
    send_out(0)
    wait_carried(1)
    finish(1)
    send_out(1)

    for r in range(2):
        first, count = RANGES[r]
        ref = w_all.at[0, pl.ds(first, count), 0, 0, pl.ds(0, 64)]
        for d in (1, 2, 3):
            wait_for(ref, wz_send.at[d, r])

        @pl.when(core == 1)
        def _():
            wait_for(ref, wz_send.at[0, r])

    @pl.when(core == 0)
    def _():
        wait_for(gains.at[0], hg_send.at[0])

    @pl.when(core == 1)
    def _():
        for s in range(2):
            wait_for(gains.at[s], hg_send.at[s])

    for u in range(4):
        ring_wait_sends(u)
    for i in range(PARTS):
        ref = token_rows(0, 0, i)
        for sem in (tok_send.at[0, i], tok_send.at[1, i], fwd_send.at[i]):
            wait_for(ref, sem)
    for s in range(2):
        for i in range(3):
            wait_for(rz.at[s, :, 0], rz_send.at[s, i])
            wait_for(rz.at[s, :, 0], cr_send.at[s, i])
    for i in range(2):
        wait_for(tp.at[pl.ds(0, 15)], a2a_send.at[i])
    for s in range(2):
        for c in range(2):
            if s == 1 and c == 0:

                @pl.when(core == 1)
                def _():
                    wait_for(outs.at[s, c], out_send.at[s, c])

            else:
                wait_for(outs.at[s, c], out_send.at[s, c])
    for p in range(4):
        wait_for(outs.at[0, 0], out_recv.at[p])


def per_device(tokens, norm_gain, norm_bias, keep_mask, projection, head_gain, traj_starts):
    any_spec = pl.BlockSpec(memory_space=pl.ANY)
    vmem = pl.BlockSpec(memory_space=pltpu.VMEM)
    dma = pltpu.SemaphoreType.DMA
    return pl.pallas_call(
        kernel,
        out_shape=jax.ShapeDtypeStruct((2048, 256), BF16),
        in_specs=[any_spec, vmem, vmem, any_spec, any_spec, vmem, pl.BlockSpec(memory_space=pltpu.SMEM)],
        out_specs=vmem,
        scratch_shapes=[
            pltpu.VMEM((OWN, D), BF16),
            pltpu.VMEM((OWN, D), I32),
            pltpu.VMEM((2, 2, OWN, D), BF16),
            pltpu.VMEM((2, 3, 4, 4, 128, 256), BF16),
            pltpu.VMEM((2, 3, 2, SPAN, 256), BF16),
            pltpu.VMEM((2, 2, SPAN, 256), F32),
            pltpu.VMEM((2, 2, 256, HEAD), BF16),
            pltpu.VMEM((2, 2, 4, 64, HEAD), BF16),
            pltpu.VMEM((8, 2, 64, HEAD), F32),
            pltpu.VMEM((128, HEAD), F32),
            pltpu.VMEM((16, 8, HEAD), F32),
            pltpu.VMEM((16, 8, HEAD), F32),
            pltpu.VMEM((128, HEAD), F32),
            pltpu.VMEM((2, 2, 4, 64, HEAD), BF16),
            pltpu.VMEM((2, 2, 256, HEAD), BF16),
            pltpu.VMEM((2, 8, 256), F32),
            pltpu.VMEM((2, 2, SPAN, 256), BF16),
            dma((2, PARTS)),
            dma((4, 2)),
            dma((2, 2, 2)),
            dma((4, 4, 2)),
            dma((4, 4, 2)),
            dma((2, PARTS)),
            dma((PARTS,)),
            dma((PARTS,)),
            dma((2, PARTS)),
            dma((2,)),
            dma((2,)),
            dma((2, 3)),
            dma((2, 4)),
            dma((2,)),
            dma((2,)),
            dma((2, 3)),
            dma((2, 4)),
            dma((2, 2)),
            dma((4,)),
        ],
        compiler_params=pltpu.CompilerParams(
            collective_id=0, has_side_effects=True, vmem_limit_bytes=48 * 1024 * 1024
        ),
    )(
        tokens, norm_gain.reshape(1, D), norm_bias.reshape(1, D), keep_mask, projection,
        jnp.broadcast_to(head_gain[None, :], (8, 256)), traj_starts,
    )


def solution(mesh):
    placed = (
        P(("outer", "inner"), None),
        P(),
        P(),
        P(("outer", "inner"), None),
        P(None, "outer", "inner"),
        P("inner"),
        P(),
    )
    return jax.shard_map(
        per_device, mesh=mesh, in_specs=placed, out_specs=P("outer", "inner"), check_vma=False
    )
```

```python
import jax
import jax.numpy as jnp
from jax import lax
from jax.experimental import pallas as pl
from jax.experimental.pallas import tpu as pltpu
from jax.sharding import PartitionSpec as P

MESH = pl.DeviceIdType.MESH
F32, BF16, I32 = jnp.float32, jnp.bfloat16, jnp.int32
D, HEAD, SPAN = 2048, 128, 512
OWN = 256
PARTS = 4
PART = OWN // PARTS
RANGES = ((1, 2), (0, 1))
UNITS = ((1, 0), (0, 0), (1, 1), (0, 1))


def slot_of(dist):
    return 1 - dist // 2


def core_of(dist):
    return ((dist + 1) // 2) % 2


def plane_at(head_plane, dist):
    up = (head_plane + dist) % 8
    down = (head_plane + 8 - dist) % 8
    return jnp.where(up % 2 == 0, up, down)


def kernel(
    tok_hbm, gain_hbm, bias_hbm, mask_hbm, proj_hbm, head_gain, traj_hbm, out,
    gain, bias, traj, tok, mask, x_all, w_all, qkv, inside, a_out, rz, local_c, t_all, tp, ps, p_all, c_out, cr, gains, outs,
    in_sem, small_sem, wz_send, wz_recv, ring_send, ring_recv, tok_send, tok_recv, fwd_send, sib_recv, hg_send, hg_recv,
    rz_send, rz_recv, a2a_send, a2a_recv, cr_send, cr_recv, out_send, out_recv,
):
    outer, z = lax.axis_index("outer"), lax.axis_index("inner")
    core, chip = outer % 2, outer // 2
    cx, cy = chip // 4, chip % 4
    pair, member = z // 2, z % 2
    along = jnp.where(core == 0, cx, cy)
    across = jnp.where(core == 0, cy, cx)

    def chip_at(a, b):
        return a * (4 - 3 * core) + b * (1 + 3 * core)

    a_next, a_prev = (along + 1) % 4, (along + 3) % 4
    b_next, b_prev = (across + 1) % 4, (across + 3) % 4

    def plane_dev(chip_id):
        return (chip_id * 2 + core, z)

    def column_dev(core_id, plane):
        return (chip * 2 + core_id, plane)

    dists = (3 - core, core)
    step = 2 * member - 1
    planes = tuple((z + step * d + 8) % 8 for d in dists)

    def remote(src, dst, send, recv, device):
        return pltpu.make_async_remote_copy(
            src_ref=src, dst_ref=dst, send_sem=send, recv_sem=recv, device_id=device, device_id_type=MESH
        )

    def wait_for(ref, sem):
        pltpu.make_async_copy(ref, ref, sem).wait()

    def in_copies(i):
        rows = pl.ds(i * PART, PART)
        return (
            pltpu.make_async_copy(tok_hbm.at[rows], tok.at[rows], in_sem.at[0, i]),
            pltpu.make_async_copy(mask_hbm.at[rows], mask.at[rows], in_sem.at[1, i]),
        )

    small_copies = (
        pltpu.make_async_copy(gain_hbm, gain, small_sem.at[0]),
        pltpu.make_async_copy(bias_hbm, bias, small_sem.at[1]),
        pltpu.make_async_copy(traj_hbm, traj, small_sem.at[2]),
    )
    for copy in in_copies(0) + small_copies:
        copy.start()
    for i in range(1, PARTS):
        for copy in in_copies(i):
            copy.start()

    barrier = pltpu.get_barrier_semaphore()

    def greet_plane(i, carry):
        pl.semaphore_signal(barrier, inc=1, device_id=plane_dev((chip + i) % 16), device_id_type=MESH)
        return carry

    def greet_column(i, carry):
        spot = (z * 2 + core + i) % 16
        pl.semaphore_signal(barrier, inc=1, device_id=column_dev(spot % 2, spot // 2), device_id_type=MESH)
        return carry

    lax.fori_loop(1, 16, greet_column, 0)
    lax.fori_loop(1, 16, greet_plane, 0)

    def wz_copy(d, r):
        first, count = RANGES[r]
        src = proj_hbm.at[pl.ds(first, count)]
        dst = w_all.at[slot_of(d), pl.ds(first, count), cx, cy, pl.ds(core * 64, 64)]
        return src, dst, wz_send.at[d, r], wz_recv.at[slot_of(d), r, core], column_dev(core_of(d), plane_at(z, d))

    def send_weights(r):
        for d in (0, 1, 2, 3):
            src, dst, send, recv, device = wz_copy(d, r)
            if d == 0:

                @pl.when(core == 0)
                def _():
                    pltpu.make_async_copy(src, dst, recv).start()

                @pl.when(core == 1)
                def _():
                    remote(src, dst, send, recv, device).start()

            else:
                remote(src, dst, send, recv, device).start()

    def send_gains():
        for d in range(4):

            @pl.when((core == core_of(d)) if d else (core == 2))
            def _():
                s = slot_of(d)
                remote(head_gain, gains.at[s], hg_send.at[s], hg_recv.at[s], column_dev(core, plane_at(z, d))).start()

        @pl.when(core == 0)
        def _():
            pltpu.make_async_copy(head_gain, gains.at[1], small_sem.at[3]).start()

    def wait_wz(u):
        s, r = UNITS[u]
        first, count = RANGES[r]
        for half in range(2):
            wait_for(w_all.at[s, pl.ds(first, count), 0, 0, pl.ds(half * 64, 64)], wz_recv.at[s, r, half])

    def block(u, chip_id, rows=None):
        s, r = UNITS[u]
        first, count = RANGES[r]
        ref = w_all.at[s, pl.ds(first, count), chip_id // 4, chip_id % 4]
        return ref if rows is None else ref.at[:, pl.ds(rows, 64)]

    def line_x(u, b, rows=None):
        s, r = UNITS[u]
        first, count = RANGES[r]
        ref = w_all.at[s, pl.ds(first, count), :, b]
        return ref if rows is None else ref.at[:, :, pl.ds(rows, 64)]

    def line_y(u, b, rows=None):
        s, r = UNITS[u]
        first, count = RANGES[r]
        ref = w_all.at[s, pl.ds(first, count), b]
        return ref if rows is None else ref.at[:, :, pl.ds(rows, 64)]

    def ring_sems(u, stage, way):
        return ring_send.at[u, stage, way], ring_recv.at[u, stage, way]

    a_devices = (plane_dev(chip_at(a_next, across)), plane_dev(chip_at(a_prev, across)))
    b_devices = (plane_dev(chip_at(along, b_next)), plane_dev(chip_at(along, b_prev)))

    def a1(u):
        wait_wz(u)
        for way in range(2):
            ref = block(u, chip)
            remote(ref, ref, *ring_sems(u, 0, way), a_devices[way]).start()

    def a_direct(u):
        wait_wz(u)
        ref = block(u, chip)
        remote(ref, ref, *ring_sems(u, 1, 0), plane_dev(chip_at((along + 2) % 4, across))).start()
        for way in range(2):
            remote(ref, ref, *ring_sems(u, 0, way), a_devices[way]).start()

    def wait_ring(u, stage):
        for way in range(2):
            ref = line_y(u, 0, 64 * way if stage == 3 else None) if stage >= 2 else block(u, 0, 64 * way if stage == 1 else None)
            wait_for(ref, ring_recv.at[u, stage, way])

    def a2(u):
        wait_ring(u, 0)
        for way in range(2):
            ref = block(u, chip_at(a_prev if way == 0 else a_next, across), 64 * way)
            remote(ref, ref, *ring_sems(u, 1, way), a_devices[way]).start()

    def b_send(u, stage, spots, halves):
        @pl.when(core == 0)
        def _():
            for way in range(2):
                ref = line_x(u, spots[way], 64 * way if halves else None)
                remote(ref, ref, *ring_sems(u, stage, way), b_devices[way]).start()

        @pl.when(core == 1)
        def _():
            for way in range(2):
                ref = line_y(u, spots[way], 64 * way if halves else None)
                remote(ref, ref, *ring_sems(u, stage, way), b_devices[way]).start()

    def b1(u):
        if u == 0:
            wait_ring(u, 0)
            wait_for(block(u, 0), ring_recv.at[u, 1, 0])
        else:
            wait_ring(u, 1)
        b_send(u, 2, (across, across), False)

    def b2(u):
        wait_ring(u, 2)
        b_send(u, 3, (b_prev, b_next), True)

    def b_done(u):
        wait_ring(u, 3)

    def ring_wait_sends(u):
        for stage in range(4):
            if u == 0 and stage == 1:
                wait_for(block(u, 0), ring_send.at[u, 1, 0])
                continue
            for way in range(2):
                half = 64 * way if stage in (1, 3) else None
                ref = line_y(u, 0, half) if stage >= 2 else block(u, 0, half)
                wait_for(ref, ring_send.at[u, stage, way])

    partner = column_dev(core, z + 1 - 2 * member)
    sibling = column_dev(1 - core, z)

    def token_rows(c, m, i):
        return x_all.at[c, m, pl.ds(i * PART, PART)]

    def normalize(i):
        for copy in in_copies(i):
            copy.wait()

        def rows16(j, carry):
            rows = pl.ds(pl.multiple_of(i * PART + j * 16, 16), 16)
            values = tok[rows, :].astype(F32)
            center = values - jnp.mean(values, axis=-1, keepdims=True)
            spread = jnp.mean(center * center, axis=-1, keepdims=True)
            scaled = center * lax.rsqrt(spread + 1e-05) * gain[...] + bias[...]
            x_all[core, member, rows, :] = (scaled * (mask[rows, :].astype(F32) * (1.0 / 0.9))).astype(BF16)
            return carry

        lax.fori_loop(0, PART // 16, rows16, 0)

    def send_tokens(i):
        ref = token_rows(core, member, i)
        remote(ref, ref, tok_send.at[0, i], tok_recv.at[i], partner).start()
        remote(ref, ref, tok_send.at[1, i], sib_recv.at[0, i], sibling).start()

    def forward_tokens(i):
        ref = token_rows(core, 1 - member, i)
        wait_for(ref, tok_recv.at[i])
        remote(ref, ref, fwd_send.at[i], sib_recv.at[1, i], sibling).start()

    def project(s, w, m):
        weights = w_all.at[s, w]

        def rows256(c, carry):
            product = jnp.dot(x_all[c, m], weights[...].reshape(D, 256), preferred_element_type=F32)
            rows = pl.ds(pl.multiple_of(m * OWN, OWN), OWN)
            qkv[s, w, c, rows, :] = product.astype(BF16)
            return carry

        lax.fori_loop(0, 2, rows256, 0)

    def start_of(position):
        first = jnp.full_like(position, -1)
        for i in range(8):
            first = jnp.where(traj[i] <= position, traj[i], first)
        return first

    def keeps(first, length):
        return jnp.where(start_of(first + (length - 1)) < first, 1.0, 0.0).astype(F32)

    chip_first = chip * 8 * SPAN

    def span_first(c):
        return chip_first + (c * 4 + pair) * SPAN

    def states(s):
        def one_span(c, carry):
            first = span_first(c)
            last_start = start_of(first + (SPAN - 1))
            spots = first + lax.broadcasted_iota(I32, (SPAN, HEAD), 0)
            kept = spots >= last_start
            for h in range(2):
                columns = slice(h * HEAD, (h + 1) * HEAD)
                values = jnp.where(kept, qkv[s, 2, c, :, columns].astype(F32), 0.0).astype(BF16)
                state = lax.dot_general(
                    qkv[s, 1, c, :, columns], values, (((0,), (0,)), ((), ())), preferred_element_type=F32
                )
                a_out[s, c, columns, :] = state.astype(BF16)
            return carry

        lax.fori_loop(0, 2, one_span, 0)

    def send_states(s):
        mine = dists[s]
        for i in range(1, 4):
            other = (mine + i) % 4
            remote(
                a_out.at[s, :, pl.ds(pl.multiple_of(other * 64, 64), 64)], rz.at[slot_of(other), :, pair],
                rz_send.at[s, i - 1], rz_recv.at[slot_of(other), pair],
                column_dev(core_of(other), plane_at(planes[s], other)),
            ).start()
        rz[s, :, pair] = a_out[s, :, pl.ds(pl.multiple_of(mine * 64, 64), 64), :]

    def wait_states(s):
        for i in range(1, 4):
            spot = (pair + i) % 4
            wait_for(rz.at[s, :, spot], rz_recv.at[s, spot])

    def chip_totals():
        for s in range(2):
            total = jnp.zeros((64, HEAD), F32)
            for j in range(8):
                local_c[j, s] = total
                total = total * keeps(chip_first + j * SPAN, SPAN) + rz[s, j // 4, j % 4].astype(F32)
            t_all[s * 64:(s + 1) * 64, :] = total

        def send(i, carry):
            other = (chip + i) % 16
            remote(
                t_all.at[pl.ds(pl.multiple_of(other * 8, 8), 8)], tp.at[chip], a2a_send.at[0], a2a_recv.at[0],
                plane_dev(other),
            ).start()
            return carry

        lax.fori_loop(1, 16, send, 0)
        tp[chip] = t_all[pl.ds(pl.multiple_of(chip * 8, 8), 8), :]

    def prefixes():
        wait_for(tp.at[pl.ds(0, 15)], a2a_recv.at[0])
        total = jnp.zeros((8, HEAD), F32)
        for k in range(16):
            ps[k] = total
            if k < 15:
                total = total * keeps(k * 8 * SPAN, 8 * SPAN) + tp[k]

        def send(i, carry):
            other = (chip + i) % 16
            remote(
                ps.at[other], p_all.at[pl.ds(pl.multiple_of(chip * 8, 8), 8)], a2a_send.at[1], a2a_recv.at[1],
                plane_dev(other),
            ).start()
            return carry

        lax.fori_loop(1, 16, send, 0)
        p_all[pl.ds(pl.multiple_of(chip * 8, 8), 8), :] = ps[chip]

    def carried():
        wait_for(tp.at[pl.ds(0, 15)], a2a_recv.at[1])
        reach = jnp.ones((), F32)
        for j in range(8):
            for s in range(2):
                total = local_c[j, s] + p_all[s * 64:(s + 1) * 64, :] * reach
                c_out[s, j // 4, j % 4] = total
            reach = reach * keeps(chip_first + j * SPAN, SPAN)
        for s in range(2):
            mine = dists[s]
            rows = pl.ds(pl.multiple_of(mine * 64, 64), 64)
            for i in range(1, 4):
                other = (mine + i) % 4
                plane = plane_at(planes[s], other)
                remote(
                    c_out.at[s, :, plane // 2], cr.at[slot_of(other), :, rows],
                    cr_send.at[s, i - 1], cr_recv.at[slot_of(other), mine],
                    column_dev(core_of(other), plane),
                ).start()
            cr[s, :, rows, :] = c_out[s, :, pair]

    def wait_carried(s):
        for i in range(1, 4):
            spot = (dists[s] + i) % 4
            wait_for(cr.at[s, :, pl.ds(0, 64)], cr_recv.at[s, spot])

    def inside_terms(s):
        def one_span(c, carry):
            first = span_first(c)
            for top in (0, 256):
                span_keys = top + 256
                rows = first + top + lax.broadcasted_iota(I32, (256, 1), 0)
                spots = first + lax.broadcasted_iota(I32, (256, span_keys), 1)
                allowed = (spots <= rows) & (spots >= start_of(rows))
                for h in range(2):
                    columns = slice(h * HEAD, (h + 1) * HEAD)
                    scores = lax.dot_general(
                        qkv[s, 0, c, top:top + 256, columns], qkv[s, 1, c, :span_keys, columns],
                        (((1,), (1,)), ((), ())), preferred_element_type=F32,
                    )
                    rounded = jnp.where(allowed, scores, 0.0).astype(BF16)
                    inside[s, c, top:top + 256, columns] = jnp.dot(
                        rounded, qkv[s, 2, c, :span_keys, columns], preferred_element_type=F32
                    )
            return carry

        lax.fori_loop(0, 2, one_span, 0)

    def finish(s, c):
        first = span_first(c)
        for top in (0, 256):
            rows = first + top + lax.broadcasted_iota(I32, (256, 1), 0)
            reached = start_of(rows) < first
            for h in range(2):
                columns = slice(h * HEAD, (h + 1) * HEAD)
                queries = qkv[s, 0, c, top:top + 256, columns]
                state = cr[s, c, columns, :]
                high = state.astype(BF16)
                low = (state - high.astype(F32)).astype(BF16)
                term = jnp.dot(queries, high, preferred_element_type=F32)
                term += jnp.dot(queries, low, preferred_element_type=F32)
                mixed = inside[s, c, top:top + 256, columns] + jnp.where(reached, term, 0.0)
                scale_back = lax.rsqrt(jnp.mean(mixed * mixed, axis=-1, keepdims=True) + 1e-06)
                outs[s, c, top:top + 256, columns] = (mixed * scale_back * gains[s, :, columns]).astype(BF16)

    def send_out(s, c):
        rows = pl.ds(pl.multiple_of(pair * SPAN, SPAN), SPAN)
        device = column_dev(c, planes[s])
        args = (outs.at[s, c], out.at[rows])
        if s == 1 and c == 0:

            @pl.when(core == 0)
            def _():
                pltpu.make_async_copy(*args, out_recv.at[pair]).start()

            @pl.when(core == 1)
            def _():
                remote(*args, out_send.at[s, c], out_recv.at[pair], device).start()

        else:
            remote(*args, out_send.at[s, c], out_recv.at[pair], device).start()

    for copy in small_copies:
        copy.wait()
    normalize(0)
    pl.semaphore_wait(barrier, 30)
    send_tokens(0)
    send_weights(0)
    normalize(1)
    send_tokens(1)
    a_direct(0)
    normalize(2)
    send_tokens(2)
    normalize(3)
    send_tokens(3)
    send_weights(1)
    send_gains()
    b1(0)
    a1(1)
    forward_tokens(0)
    a2(1)
    b2(0)
    b1(1)
    forward_tokens(1)
    a1(2)
    a1(3)
    b_done(0)
    for i in range(PARTS):
        wait_for(token_rows(1 - core, member, i), sib_recv.at[0, i])
    for w in (1, 2):
        project(1, w, member)
    forward_tokens(2)
    a2(2)
    a2(3)
    b2(1)
    forward_tokens(3)
    b1(2)
    b1(3)
    for i in range(PARTS):
        wait_for(token_rows(1 - core, 1 - member, i), sib_recv.at[1, i])
    for w in (1, 2):
        project(1, w, 1 - member)
    states(1)
    send_states(1)
    b_done(1)
    for w in (1, 2):
        project(0, w, member)
        project(0, w, 1 - member)
    states(0)
    send_states(0)
    b2(2)
    wait_states(1)
    wait_states(0)
    chip_totals()
    b2(3)
    b_done(2)
    for m in range(2):
        project(1, 0, m)
    prefixes()
    b_done(3)
    for m in range(2):
        project(0, 0, m)
    carried()
    inside_terms(0)
    inside_terms(1)

    @pl.when(core == 0)
    def _():
        wait_for(gains.at[0], hg_recv.at[0])
        wait_for(gains.at[1], small_sem.at[3])

    @pl.when(core == 1)
    def _():
        for s in range(2):
            wait_for(gains.at[s], hg_recv.at[s])

    for s in range(2):
        wait_carried(s)
        for c in range(2):
            finish(s, c)
            send_out(s, c)

    for r in range(2):
        first, count = RANGES[r]
        ref = w_all.at[0, pl.ds(first, count), 0, 0, pl.ds(0, 64)]
        for d in (1, 2, 3):
            wait_for(ref, wz_send.at[d, r])

        @pl.when(core == 1)
        def _():
            wait_for(ref, wz_send.at[0, r])

    @pl.when(core == 0)
    def _():
        wait_for(gains.at[0], hg_send.at[0])

    @pl.when(core == 1)
    def _():
        for s in range(2):
            wait_for(gains.at[s], hg_send.at[s])

    for u in range(4):
        ring_wait_sends(u)
    for i in range(PARTS):
        ref = token_rows(0, 0, i)
        for sem in (tok_send.at[0, i], tok_send.at[1, i], fwd_send.at[i]):
            wait_for(ref, sem)
    for s in range(2):
        for i in range(3):
            wait_for(rz.at[s, :, 0], rz_send.at[s, i])
            wait_for(c_out.at[s, :, 0], cr_send.at[s, i])
    for i in range(2):
        wait_for(tp.at[pl.ds(0, 15)], a2a_send.at[i])
    for s in range(2):
        for c in range(2):
            if s == 1 and c == 0:

                @pl.when(core == 1)
                def _():
                    wait_for(outs.at[s, c], out_send.at[s, c])

            else:
                wait_for(outs.at[s, c], out_send.at[s, c])
    for p in range(4):
        wait_for(outs.at[0, 0], out_recv.at[p])


def per_device(tokens, norm_gain, norm_bias, keep_mask, projection, head_gain, traj_starts):
    any_spec = pl.BlockSpec(memory_space=pl.ANY)
    vmem = pl.BlockSpec(memory_space=pltpu.VMEM)
    dma = pltpu.SemaphoreType.DMA
    return pl.pallas_call(
        kernel,
        out_shape=jax.ShapeDtypeStruct((2048, 256), BF16),
        in_specs=[any_spec] * 7,
        out_specs=vmem,
        scratch_shapes=[
            pltpu.VMEM((1, D), F32),
            pltpu.VMEM((1, D), F32),
            pltpu.SMEM((8,), I32),
            pltpu.VMEM((OWN, D), BF16),
            pltpu.VMEM((OWN, D), I32),
            pltpu.VMEM((2, 2, OWN, D), BF16),
            pltpu.VMEM((2, 3, 4, 4, 128, 256), BF16),
            pltpu.VMEM((2, 3, 2, SPAN, 256), BF16),
            pltpu.VMEM((2, 2, SPAN, 256), F32),
            pltpu.VMEM((2, 2, 256, HEAD), BF16),
            pltpu.VMEM((2, 2, 4, 64, HEAD), BF16),
            pltpu.VMEM((8, 2, 64, HEAD), F32),
            pltpu.VMEM((128, HEAD), F32),
            pltpu.VMEM((16, 8, HEAD), F32),
            pltpu.VMEM((16, 8, HEAD), F32),
            pltpu.VMEM((128, HEAD), F32),
            pltpu.VMEM((2, 2, 4, 64, HEAD), F32),
            pltpu.VMEM((2, 2, 256, HEAD), F32),
            pltpu.VMEM((2, 1, 256), F32),
            pltpu.VMEM((2, 2, SPAN, 256), BF16),
            dma((2, PARTS)),
            dma((4,)),
            dma((4, 2)),
            dma((2, 2, 2)),
            dma((4, 4, 2)),
            dma((4, 4, 2)),
            dma((2, PARTS)),
            dma((PARTS,)),
            dma((PARTS,)),
            dma((2, PARTS)),
            dma((2,)),
            dma((2,)),
            dma((2, 3)),
            dma((2, 4)),
            dma((2,)),
            dma((2,)),
            dma((2, 3)),
            dma((2, 4)),
            dma((2, 2)),
            dma((4,)),
        ],
        compiler_params=pltpu.CompilerParams(
            collective_id=0, has_side_effects=True, vmem_limit_bytes=63 * 1024 * 1024
        ),
    )(
        tokens, norm_gain.reshape(1, D), norm_bias.reshape(1, D), keep_mask, projection,
        head_gain.reshape(1, 256), traj_starts,
    )


def solution(mesh):
    placed = (
        P(("outer", "inner"), None),
        P(),
        P(),
        P(("outer", "inner"), None),
        P(None, "outer", "inner"),
        P("inner"),
        P(),
    )
    return jax.shard_map(
        per_device, mesh=mesh, in_specs=placed, out_specs=P("outer", "inner"), check_vma=False
    )
```

```python
import jax
import jax.numpy as jnp
from jax import lax
from jax.experimental import pallas as pl
from jax.experimental.pallas import tpu as pltpu
from jax.sharding import PartitionSpec as P

MESH = pl.DeviceIdType.MESH
F32, BF16, I32 = jnp.float32, jnp.bfloat16, jnp.int32
D, HEAD, SPAN = 2048, 128, 512
OWN = 256
DIRECT = 2
PARTS = 4
PART = OWN // PARTS
QUERY, KEY, VALUE = 0, 1, 2
UNITS = ((1, KEY), (1, VALUE), (0, KEY), (0, VALUE), (1, QUERY), (0, QUERY))


def slot_of(dist):
    return 1 - dist // 2


def core_of(dist):
    return ((dist + 1) // 2) % 2


def plane_at(head_plane, dist):
    up = (head_plane + dist) % 8
    down = (head_plane + 8 - dist) % 8
    return jnp.where(up % 2 == 0, up, down)


def kernel(
    tok_hbm, gain_hbm, bias_hbm, mask_hbm, proj_hbm, head_gain, traj_hbm, out,
    gain, bias, traj, tok, mask, x_all, w_all, qkv, inside, a_out, rz, local_c, t_all, tp, ps, local_in, prefix_in, gains, outs,
    in_sem, small_sem, wz_send, wz_recv, ring_send, ring_recv, tok_send, tok_recv, fwd_send, sib_recv, hg_send, hg_recv,
    rz_send, rz_recv, a2a_send, a2a_recv, local_send, local_recv, prefix_send, prefix_recv, out_send, out_recv,
):
    outer, z = lax.axis_index("outer"), lax.axis_index("inner")
    core, chip = outer % 2, outer // 2
    cx, cy = chip // 4, chip % 4
    pair, member = z // 2, z % 2
    along = jnp.where(core == 0, cx, cy)
    across = jnp.where(core == 0, cy, cx)

    def chip_at(a, b):
        return a * (4 - 3 * core) + b * (1 + 3 * core)

    a_next, a_prev = (along + 1) % 4, (along + 3) % 4
    b_next, b_prev = (across + 1) % 4, (across + 3) % 4

    def plane_dev(chip_id):
        return (chip_id * 2 + core, z)

    def column_dev(core_id, plane):
        return (chip * 2 + core_id, plane)

    dists = (3 - core, core)
    step = 2 * member - 1
    planes = tuple((z + step * d + 8) % 8 for d in dists)

    def remote(src, dst, send, recv, device):
        return pltpu.make_async_remote_copy(
            src_ref=src, dst_ref=dst, send_sem=send, recv_sem=recv, device_id=device, device_id_type=MESH
        )

    def wait_for(ref, sem):
        pltpu.make_async_copy(ref, ref, sem).wait()

    sixty_three = prefix_in.at[pl.ds(0, 63)]

    def in_copies(i):
        rows = pl.ds(i * PART, PART)
        return (
            pltpu.make_async_copy(tok_hbm.at[rows], tok.at[rows], in_sem.at[0, i]),
            pltpu.make_async_copy(mask_hbm.at[rows], mask.at[rows], in_sem.at[1, i]),
        )

    small_copies = (
        pltpu.make_async_copy(gain_hbm, gain, small_sem.at[0]),
        pltpu.make_async_copy(bias_hbm, bias, small_sem.at[1]),
        pltpu.make_async_copy(traj_hbm, traj, small_sem.at[2]),
    )
    for copy in in_copies(0) + small_copies:
        copy.start()
    for i in range(1, PARTS):
        for copy in in_copies(i):
            copy.start()

    barrier = pltpu.get_barrier_semaphore()

    def greet_plane(i, carry):
        pl.semaphore_signal(barrier, inc=1, device_id=plane_dev((chip + i) % 16), device_id_type=MESH)
        return carry

    def greet_column(i, carry):
        spot = (z * 2 + core + i) % 16
        pl.semaphore_signal(barrier, inc=1, device_id=column_dev(spot % 2, spot // 2), device_id_type=MESH)
        return carry

    lax.fori_loop(1, 16, greet_column, 0)
    lax.fori_loop(1, 16, greet_plane, 0)

    def wz_copy(d, w):
        src = proj_hbm.at[w]
        dst = w_all.at[slot_of(d), w, cx, cy, pl.ds(core * 64, 64)]
        return src, dst, wz_send.at[d, w], wz_recv.at[slot_of(d), w, core], column_dev(core_of(d), plane_at(z, d))

    def send_weights(w, which):
        for d in which:
            src, dst, send, recv, device = wz_copy(d, w)
            if d == 0:

                @pl.when(core == 0)
                def _():
                    pltpu.make_async_copy(src, dst, recv).start()

                @pl.when(core == 1)
                def _():
                    remote(src, dst, send, recv, device).start()

            else:
                remote(src, dst, send, recv, device).start()

    def send_gains():
        for d in range(4):

            @pl.when((core == core_of(d)) if d else (core == 2))
            def _():
                s = slot_of(d)
                remote(head_gain, gains.at[s], hg_send.at[s], hg_recv.at[s], column_dev(core, plane_at(z, d))).start()

        @pl.when(core == 0)
        def _():
            pltpu.make_async_copy(head_gain, gains.at[1], small_sem.at[3]).start()

    def wait_wz(u):
        s, w = UNITS[u]
        for half in range(2):
            wait_for(w_all.at[s, w, 0, 0, pl.ds(half * 64, 64)], wz_recv.at[s, w, half])

    def block(u, chip_id, rows=None):
        ref = w_all.at[(*UNITS[u], chip_id // 4, chip_id % 4)]
        return ref if rows is None else ref.at[pl.ds(rows, 64)]

    def line_x(u, b, rows=None):
        ref = w_all.at[(*UNITS[u], slice(None), b)]
        return ref if rows is None else ref.at[:, pl.ds(rows, 64)]

    def line_y(u, b, rows=None):
        ref = w_all.at[(*UNITS[u], b)]
        return ref if rows is None else ref.at[:, pl.ds(rows, 64)]

    def ring_sems(u, stage, way):
        return ring_send.at[u, stage, way], ring_recv.at[u, stage, way]

    a_devices = (plane_dev(chip_at(a_next, across)), plane_dev(chip_at(a_prev, across)))
    b_devices = (plane_dev(chip_at(along, b_next)), plane_dev(chip_at(along, b_prev)))

    def a1(u):
        wait_wz(u)
        for way in range(2):
            ref = block(u, chip)
            remote(ref, ref, *ring_sems(u, 0, way), a_devices[way]).start()

    def a_direct(u):
        wait_wz(u)
        ref = block(u, chip)
        remote(ref, ref, *ring_sems(u, 1, 0), plane_dev(chip_at((along + 2) % 4, across))).start()
        for way in range(2):
            remote(ref, ref, *ring_sems(u, 0, way), a_devices[way]).start()

    def wait_ring(u, stage):
        for way in range(2):
            ref = line_y(u, 0, 64 * way if stage == 3 else None) if stage >= 2 else block(u, 0, 64 * way if stage == 1 else None)
            wait_for(ref, ring_recv.at[u, stage, way])

    def a2(u):
        wait_ring(u, 0)
        for way in range(2):
            ref = block(u, chip_at(a_prev if way == 0 else a_next, across), 64 * way)
            remote(ref, ref, *ring_sems(u, 1, way), a_devices[way]).start()

    def b_send(u, stage, spots, halves):
        @pl.when(core == 0)
        def _():
            for way in range(2):
                ref = line_x(u, spots[way], 64 * way if halves else None)
                remote(ref, ref, *ring_sems(u, stage, way), b_devices[way]).start()

        @pl.when(core == 1)
        def _():
            for way in range(2):
                ref = line_y(u, spots[way], 64 * way if halves else None)
                remote(ref, ref, *ring_sems(u, stage, way), b_devices[way]).start()

    def b1(u):
        if u < DIRECT:
            wait_ring(u, 0)
            wait_for(block(u, 0), ring_recv.at[u, 1, 0])
        else:
            wait_ring(u, 1)
        b_send(u, 2, (across, across), False)

    def b2(u):
        wait_ring(u, 2)
        b_send(u, 3, (b_prev, b_next), True)

    def b_done(u):
        wait_ring(u, 3)

    def ring_wait_sends(u):
        for stage in range(4):
            if u < DIRECT and stage == 1:
                wait_for(block(u, 0), ring_send.at[u, 1, 0])
                continue
            for way in range(2):
                half = 64 * way if stage in (1, 3) else None
                ref = line_y(u, 0, half) if stage >= 2 else block(u, 0, half)
                wait_for(ref, ring_send.at[u, stage, way])

    partner = column_dev(core, z + 1 - 2 * member)
    sibling = column_dev(1 - core, z)

    def token_rows(c, m, i):
        return x_all.at[c, m, pl.ds(i * PART, PART)]

    def normalize(i):
        for copy in in_copies(i):
            copy.wait()

        def rows16(j, carry):
            rows = pl.ds(pl.multiple_of(i * PART + j * 16, 16), 16)
            values = tok[rows, :].astype(F32)
            center = values - jnp.mean(values, axis=-1, keepdims=True)
            spread = jnp.mean(center * center, axis=-1, keepdims=True)
            scaled = center * lax.rsqrt(spread + 1e-05) * gain[...] + bias[...]
            x_all[core, member, rows, :] = (scaled * (mask[rows, :].astype(F32) * (1.0 / 0.9))).astype(BF16)
            return carry

        lax.fori_loop(0, PART // 16, rows16, 0)

    def send_tokens(i):
        ref = token_rows(core, member, i)
        remote(ref, ref, tok_send.at[0, i], tok_recv.at[i], partner).start()
        remote(ref, ref, tok_send.at[1, i], sib_recv.at[0, i], sibling).start()

    def forward_tokens(i):
        ref = token_rows(core, 1 - member, i)
        wait_for(ref, tok_recv.at[i])
        remote(ref, ref, fwd_send.at[i], sib_recv.at[1, i], sibling).start()

    def project(s, w, m):
        weights = w_all.at[s, w]

        def rows256(c, carry):
            product = jnp.dot(x_all[c, m], weights[...].reshape(D, 256), preferred_element_type=F32)
            rows = pl.ds(pl.multiple_of(m * OWN, OWN), OWN)
            qkv[s, w, c, rows, :] = product.astype(BF16)
            return carry

        lax.fori_loop(0, 2, rows256, 0)

    def start_of(position):
        first = jnp.full_like(position, -1)
        for i in range(8):
            first = jnp.where(traj[i] <= position, traj[i], first)
        return first

    def keeps(first, length):
        return jnp.where(start_of(first + (length - 1)) < first, 1.0, 0.0).astype(F32)

    chip_first = chip * 8 * SPAN

    def span_first(c):
        return chip_first + (c * 4 + pair) * SPAN

    def states(s):
        def one_span(c, carry):
            first = span_first(c)
            last_start = start_of(first + (SPAN - 1))
            spots = first + lax.broadcasted_iota(I32, (SPAN, HEAD), 0)
            kept = spots >= last_start
            for h in range(2):
                columns = slice(h * HEAD, (h + 1) * HEAD)
                values = jnp.where(kept, qkv[s, 2, c, :, columns].astype(F32), 0.0).astype(BF16)
                state = lax.dot_general(
                    qkv[s, 1, c, :, columns], values, (((0,), (0,)), ((), ())), preferred_element_type=F32
                )
                a_out[s, c, columns, :] = state.astype(BF16)
            return carry

        lax.fori_loop(0, 2, one_span, 0)

    def send_states(s):
        mine = dists[s]
        for i in range(1, 4):
            other = (mine + i) % 4
            remote(
                a_out.at[s, :, pl.ds(pl.multiple_of(other * 64, 64), 64)], rz.at[slot_of(other), :, pair],
                rz_send.at[s, i - 1], rz_recv.at[slot_of(other), pair],
                column_dev(core_of(other), plane_at(planes[s], other)),
            ).start()
        rz[s, :, pair] = a_out[s, :, pl.ds(pl.multiple_of(mine * 64, 64), 64), :]

    def wait_states(s):
        for i in range(1, 4):
            spot = (pair + i) % 4
            wait_for(rz.at[s, :, spot], rz_recv.at[s, spot])

    def chip_totals():
        for s in range(2):
            total = jnp.zeros((64, HEAD), F32)
            for j in range(8):
                local_c[s, j // 4, j % 4] = total
                total = total * keeps(chip_first + j * SPAN, SPAN) + rz[s, j // 4, j % 4].astype(F32)
            t_all[s * 64:(s + 1) * 64, :] = total

        def send(i, carry):
            other = (chip + i) % 16
            remote(
                t_all.at[pl.ds(pl.multiple_of(other * 8, 8), 8)], tp.at[chip], a2a_send, a2a_recv, plane_dev(other)
            ).start()
            return carry

        lax.fori_loop(1, 16, send, 0)
        tp[chip] = t_all[pl.ds(pl.multiple_of(chip * 8, 8), 8), :]

    def send_local():
        for s in range(2):
            mine = dists[s]
            rows = pl.ds(pl.multiple_of(mine * 64, 64), 64)
            for i in range(1, 4):
                other = (mine + i) % 4
                plane = plane_at(planes[s], other)
                remote(
                    local_c.at[s, :, plane // 2], local_in.at[slot_of(other), :, rows],
                    local_send.at[s, i - 1], local_recv.at[slot_of(other), mine],
                    column_dev(core_of(other), plane),
                ).start()
            local_in[s, :, rows, :] = local_c[s, :, pair]

    def prefixes():
        wait_for(tp.at[pl.ds(0, 15)], a2a_recv)
        total = jnp.zeros((8, HEAD), F32)
        for k in range(16):
            ps[k] = total
            if k < 15:
                total = total * keeps(k * 8 * SPAN, 8 * SPAN) + tp[k]
        slot = chip // 8
        mine = jnp.where(slot == 0, dists[0], dists[1])
        head_plane = jnp.where(slot == 0, planes[0], planes[1])
        spot = mine * 8 + chip % 8

        def to_chip(i, carry):
            other = (chip + i) % 16
            for near in range(4):
                dist = (mine + near) % 4
                plane = plane_at(head_plane, dist)
                target = (other * 2 + core_of(dist), plane)
                if near == 0:

                    @pl.when(i != 0)
                    def _():
                        remote(
                            ps.at[other], prefix_in.at[slot_of(dist) * 32 + spot], prefix_send, prefix_recv, target
                        ).start()
                else:
                    remote(
                        ps.at[other], prefix_in.at[slot_of(dist) * 32 + spot], prefix_send, prefix_recv, target
                    ).start()
            return carry

        lax.fori_loop(0, 16, to_chip, 0)
        prefix_in[slot * 32 + spot] = ps[chip]

    def wait_prefix():
        wait_for(sixty_three, prefix_recv)

    def wait_local(s):
        for i in range(1, 4):
            spot = (dists[s] + i) % 4
            wait_for(local_in.at[s, :, pl.ds(0, 64)], local_recv.at[s, spot])

    def inside_terms(s):
        def one_span(c, carry):
            first = span_first(c)
            for top in (0, 256):
                span_keys = top + 256
                rows = first + top + lax.broadcasted_iota(I32, (256, 1), 0)
                spots = first + lax.broadcasted_iota(I32, (256, span_keys), 1)
                allowed = (spots <= rows) & (spots >= start_of(rows))
                for h in range(2):
                    columns = slice(h * HEAD, (h + 1) * HEAD)
                    scores = lax.dot_general(
                        qkv[s, 0, c, top:top + 256, columns], qkv[s, 1, c, :span_keys, columns],
                        (((1,), (1,)), ((), ())), preferred_element_type=F32,
                    )
                    rounded = jnp.where(allowed, scores, 0.0).astype(BF16)
                    inside[s, c, top:top + 256, columns] = jnp.dot(
                        rounded, qkv[s, 2, c, :span_keys, columns], preferred_element_type=F32
                    )
            return carry

        lax.fori_loop(0, 2, one_span, 0)

    def finish(s, c):
        first = span_first(c)
        reach = jnp.ones((), F32)
        for j in range(7):
            going_on = reach * keeps(chip_first + j * SPAN, SPAN)
            reach = jnp.where(j < c * 4 + pair, going_on, reach)
        for top in (0, 256):
            rows = first + top + lax.broadcasted_iota(I32, (256, 1), 0)
            reached = start_of(rows) < first
            for h in range(2):
                columns = slice(h * HEAD, (h + 1) * HEAD)
                queries = qkv[s, 0, c, top:top + 256, columns]
                prefix = prefix_in[s * 32 + h * 16:s * 32 + (h + 1) * 16].reshape(HEAD, HEAD)
                state = local_in[s, c, columns, :] + prefix * reach
                high = state.astype(BF16)
                low = (state - high.astype(F32)).astype(BF16)
                term = jnp.dot(queries, high, preferred_element_type=F32)
                term += jnp.dot(queries, low, preferred_element_type=F32)
                mixed = inside[s, c, top:top + 256, columns] + jnp.where(reached, term, 0.0)
                scale_back = lax.rsqrt(jnp.mean(mixed * mixed, axis=-1, keepdims=True) + 1e-06)
                outs[s, c, top:top + 256, columns] = (mixed * scale_back * gains[s, :, columns]).astype(BF16)

    def send_out(s, c):
        rows = pl.ds(pl.multiple_of(pair * SPAN, SPAN), SPAN)
        device = column_dev(c, planes[s])
        args = (outs.at[s, c], out.at[rows])
        if s == 1 and c == 0:

            @pl.when(core == 0)
            def _():
                pltpu.make_async_copy(*args, out_recv.at[pair]).start()

            @pl.when(core == 1)
            def _():
                remote(*args, out_send.at[s, c], out_recv.at[pair], device).start()

        else:
            remote(*args, out_send.at[s, c], out_recv.at[pair], device).start()

    for copy in small_copies:
        copy.wait()
    normalize(0)
    pl.semaphore_wait(barrier, 30)
    send_tokens(0)
    send_weights(KEY, (0, 1))
    send_weights(VALUE, (0, 1))
    send_weights(KEY, (3, 2))
    send_weights(VALUE, (3, 2))
    normalize(1)
    send_tokens(1)
    normalize(2)
    send_tokens(2)
    a_direct(0)
    normalize(3)
    send_tokens(3)
    a_direct(1)
    send_weights(QUERY, (0, 1, 2, 3))
    send_gains()
    b1(0)
    a1(2)
    b1(1)
    a1(3)
    forward_tokens(0)
    a2(2)
    b2(0)
    a2(3)
    b1(2)
    forward_tokens(1)
    b2(1)
    a1(4)
    b_done(0)
    for i in range(PARTS):
        wait_for(token_rows(1 - core, member, i), sib_recv.at[0, i])
    project(1, KEY, member)
    b1(3)
    a1(5)
    b_done(1)
    project(1, VALUE, member)
    forward_tokens(2)
    b2(2)
    a2(4)
    b1(4)
    b2(3)
    a2(5)
    b_done(2)
    project(0, KEY, member)
    forward_tokens(3)
    b1(5)
    for i in range(PARTS):
        wait_for(token_rows(1 - core, 1 - member, i), sib_recv.at[1, i])
    project(1, KEY, 1 - member)
    project(1, VALUE, 1 - member)
    states(1)
    send_states(1)
    project(0, KEY, 1 - member)
    b_done(3)
    project(0, VALUE, member)
    project(0, VALUE, 1 - member)
    states(0)
    send_states(0)
    b2(4)
    b2(5)
    wait_states(1)
    wait_states(0)
    chip_totals()
    send_local()
    b_done(4)
    for m in range(2):
        project(1, QUERY, m)
    prefixes()
    b_done(5)
    for m in range(2):
        project(0, QUERY, m)
    inside_terms(0)
    inside_terms(1)

    @pl.when(core == 0)
    def _():
        wait_for(gains.at[0], hg_recv.at[0])
        wait_for(gains.at[1], small_sem.at[3])

    @pl.when(core == 1)
    def _():
        for s in range(2):
            wait_for(gains.at[s], hg_recv.at[s])

    wait_local(0)
    wait_local(1)
    wait_prefix()
    for s in range(2):
        for c in range(2):
            finish(s, c)
            send_out(s, c)

    ref = w_all.at[0, 0, 0, 0, pl.ds(0, 64)]
    for w in range(3):
        for d in (1, 2, 3):
            wait_for(ref, wz_send.at[d, w])

    @pl.when(core == 1)
    def _():
        for w in range(3):
            wait_for(ref, wz_send.at[0, w])

    @pl.when(core == 0)
    def _():
        wait_for(gains.at[0], hg_send.at[0])

    @pl.when(core == 1)
    def _():
        for s in range(2):
            wait_for(gains.at[s], hg_send.at[s])

    for u in range(len(UNITS)):
        ring_wait_sends(u)
    for i in range(PARTS):
        ref = token_rows(0, 0, i)
        for sem in (tok_send.at[0, i], tok_send.at[1, i], fwd_send.at[i]):
            wait_for(ref, sem)
    for s in range(2):
        for i in range(3):
            wait_for(rz.at[s, :, 0], rz_send.at[s, i])
            wait_for(local_c.at[s, :, 0], local_send.at[s, i])
    wait_for(tp.at[pl.ds(0, 15)], a2a_send)
    wait_for(sixty_three, prefix_send)
    for s in range(2):
        for c in range(2):
            if s == 1 and c == 0:

                @pl.when(core == 1)
                def _():
                    wait_for(outs.at[s, c], out_send.at[s, c])

            else:
                wait_for(outs.at[s, c], out_send.at[s, c])
    for p in range(4):
        wait_for(outs.at[0, 0], out_recv.at[p])


def per_device(tokens, norm_gain, norm_bias, keep_mask, projection, head_gain, traj_starts):
    any_spec = pl.BlockSpec(memory_space=pl.ANY)
    dma = pltpu.SemaphoreType.DMA
    return pl.pallas_call(
        kernel,
        out_shape=jax.ShapeDtypeStruct((2048, 256), BF16),
        in_specs=[any_spec] * 7,
        out_specs=any_spec,
        scratch_shapes=[
            pltpu.VMEM((1, D), F32),
            pltpu.VMEM((1, D), F32),
            pltpu.SMEM((8,), I32),
            pltpu.VMEM((OWN, D), BF16),
            pltpu.VMEM((OWN, D), I32),
            pltpu.VMEM((2, 2, OWN, D), BF16),
            pltpu.VMEM((2, 3, 4, 4, 128, 256), BF16),
            pltpu.VMEM((2, 3, 2, SPAN, 256), BF16),
            pltpu.VMEM((2, 2, SPAN, 256), F32),
            pltpu.VMEM((2, 2, 256, HEAD), BF16),
            pltpu.VMEM((2, 2, 4, 64, HEAD), BF16),
            pltpu.VMEM((2, 2, 4, 64, HEAD), F32),
            pltpu.VMEM((128, HEAD), F32),
            pltpu.VMEM((16, 8, HEAD), F32),
            pltpu.VMEM((16, 8, HEAD), F32),
            pltpu.VMEM((2, 2, 256, HEAD), F32),
            pltpu.VMEM((64, 8, HEAD), F32),
            pltpu.VMEM((2, 1, 256), F32),
            pltpu.VMEM((2, 2, SPAN, 256), BF16),
            dma((2, PARTS)),
            dma((4,)),
            dma((4, 3)),
            dma((2, 3, 2)),
            dma((len(UNITS), 4, 2)),
            dma((len(UNITS), 4, 2)),
            dma((2, PARTS)),
            dma((PARTS,)),
            dma((PARTS,)),
            dma((2, PARTS)),
            dma((2,)),
            dma((2,)),
            dma((2, 3)),
            dma((2, 4)),
            dma(()),
            dma(()),
            dma((2, 3)),
            dma((2, 4)),
            dma(()),
            dma(()),
            dma((2, 2)),
            dma((4,)),
        ],
        compiler_params=pltpu.CompilerParams(
            collective_id=0, has_side_effects=True, vmem_limit_bytes=63 * 1024 * 1024
        ),
    )(
        tokens, norm_gain.reshape(1, D), norm_bias.reshape(1, D), keep_mask, projection,
        head_gain.reshape(1, 256), traj_starts,
    )


def solution(mesh):
    placed = (
        P(("outer", "inner"), None),
        P(),
        P(),
        P(("outer", "inner"), None),
        P(None, "outer", "inner"),
        P("inner"),
        P(),
    )
    return jax.shard_map(
        per_device, mesh=mesh, in_specs=placed, out_specs=P("outer", "inner"), check_vma=False
    )
```

```python
import jax
import jax.numpy as jnp
from jax import lax
from jax.experimental import pallas as pl
from jax.experimental.pallas import tpu as pltpu
from jax.sharding import PartitionSpec as P

MESH = pl.DeviceIdType.MESH
F32, BF16, I32 = jnp.float32, jnp.bfloat16, jnp.int32
D, HEAD, SPAN = 2048, 128, 512
OWN = 256
DIRECT = 1
PARTS = 4
PART = OWN // PARTS
QUERY, KEY, VALUE = 0, 1, 2
UNITS = ((1, KEY), (0, KEY), (0, VALUE), (1, VALUE), (0, QUERY), (1, QUERY))


def slot_of(dist):
    return 1 - dist // 2


def core_of(dist):
    return ((dist + 1) // 2) % 2


def plane_at(head_plane, dist):
    up = (head_plane + dist) % 8
    down = (head_plane + 8 - dist) % 8
    return jnp.where(up % 2 == 0, up, down)


def kernel(
    tok_hbm, gain_hbm, bias_hbm, mask_hbm, proj_hbm, head_gain, traj_hbm, out,
    gain, bias, traj, tok, mask, x_all, w_all, qkv, inside, a_out, rz, local_c, t_all, tp, ps, local_in, prefix_in, gains, outs,
    in_sem, small_sem, wz_send, wz_recv, ring_send, ring_recv, tok_send, tok_recv, fwd_send, sib_recv, hg_send, hg_recv,
    rz_send, rz_recv, a2a_send, a2a_recv, local_send, local_recv, prefix_send, prefix_recv, out_send, out_recv,
):
    outer, z = lax.axis_index("outer"), lax.axis_index("inner")
    core, chip = outer % 2, outer // 2
    cx, cy = chip // 4, chip % 4
    pair, member = z // 2, z % 2
    along = jnp.where(core == 0, cx, cy)
    across = jnp.where(core == 0, cy, cx)

    def chip_at(a, b):
        return a * (4 - 3 * core) + b * (1 + 3 * core)

    a_next, a_prev = (along + 1) % 4, (along + 3) % 4
    b_next, b_prev = (across + 1) % 4, (across + 3) % 4

    def plane_dev(chip_id):
        return (chip_id * 2 + core, z)

    def column_dev(core_id, plane):
        return (chip * 2 + core_id, plane)

    dists = (3 - core, core)
    step = 2 * member - 1
    planes = tuple((z + step * d + 8) % 8 for d in dists)

    def remote(src, dst, send, recv, device):
        return pltpu.make_async_remote_copy(
            src_ref=src, dst_ref=dst, send_sem=send, recv_sem=recv, device_id=device, device_id_type=MESH
        )

    def wait_for(ref, sem):
        pltpu.make_async_copy(ref, ref, sem).wait()

    def in_copies(i):
        rows = pl.ds(i * PART, PART)
        return (
            pltpu.make_async_copy(tok_hbm.at[rows], tok.at[rows], in_sem.at[0, i]),
            pltpu.make_async_copy(mask_hbm.at[rows], mask.at[rows], in_sem.at[1, i]),
        )

    small_copies = (
        pltpu.make_async_copy(gain_hbm, gain, small_sem.at[0]),
        pltpu.make_async_copy(bias_hbm, bias, small_sem.at[1]),
        pltpu.make_async_copy(traj_hbm, traj, small_sem.at[2]),
    )
    for copy in in_copies(0) + small_copies:
        copy.start()
    for i in range(1, PARTS):
        for copy in in_copies(i):
            copy.start()

    barrier = pltpu.get_barrier_semaphore()

    def greet_plane(i, carry):
        pl.semaphore_signal(barrier, inc=1, device_id=plane_dev((chip + i) % 16), device_id_type=MESH)
        return carry

    def greet_column(i, carry):
        spot = (z * 2 + core + i) % 16
        pl.semaphore_signal(barrier, inc=1, device_id=column_dev(spot % 2, spot // 2), device_id_type=MESH)
        return carry

    lax.fori_loop(1, 16, greet_column, 0)
    lax.fori_loop(1, 16, greet_plane, 0)

    def wz_copy(d, w):
        src = proj_hbm.at[w]
        dst = w_all.at[slot_of(d), w, cx, cy, pl.ds(core * 64, 64)]
        return src, dst, wz_send.at[d, w], wz_recv.at[slot_of(d), w, core], column_dev(core_of(d), plane_at(z, d))

    def send_weights(w, which):
        for d in which:
            src, dst, send, recv, device = wz_copy(d, w)
            if d == 0:

                @pl.when(core == 0)
                def _():
                    pltpu.make_async_copy(src, dst, recv).start()

                @pl.when(core == 1)
                def _():
                    remote(src, dst, send, recv, device).start()

            else:
                remote(src, dst, send, recv, device).start()

    def send_gains():
        for d in range(4):

            @pl.when((core == core_of(d)) if d else (core == 2))
            def _():
                s = slot_of(d)
                remote(head_gain, gains.at[s], hg_send.at[s], hg_recv.at[s], column_dev(core, plane_at(z, d))).start()

        @pl.when(core == 0)
        def _():
            pltpu.make_async_copy(head_gain, gains.at[1], small_sem.at[3]).start()

    def wait_wz(u):
        s, w = UNITS[u]
        for half in range(2):
            wait_for(w_all.at[s, w, 0, 0, pl.ds(half * 64, 64)], wz_recv.at[s, w, half])

    def block(u, chip_id, rows=None):
        ref = w_all.at[(*UNITS[u], chip_id // 4, chip_id % 4)]
        return ref if rows is None else ref.at[pl.ds(rows, 64)]

    def line_x(u, b, rows=None):
        ref = w_all.at[(*UNITS[u], slice(None), b)]
        return ref if rows is None else ref.at[:, pl.ds(rows, 64)]

    def line_y(u, b, rows=None):
        ref = w_all.at[(*UNITS[u], b)]
        return ref if rows is None else ref.at[:, pl.ds(rows, 64)]

    def ring_sems(u, stage, way):
        return ring_send.at[u, stage, way], ring_recv.at[u, stage, way]

    a_devices = (plane_dev(chip_at(a_next, across)), plane_dev(chip_at(a_prev, across)))
    b_devices = (plane_dev(chip_at(along, b_next)), plane_dev(chip_at(along, b_prev)))

    def a1(u):
        wait_wz(u)
        for way in range(2):
            ref = block(u, chip)
            remote(ref, ref, *ring_sems(u, 0, way), a_devices[way]).start()

    def a_direct(u):
        wait_wz(u)
        ref = block(u, chip)
        remote(ref, ref, *ring_sems(u, 1, 0), plane_dev(chip_at((along + 2) % 4, across))).start()
        for way in range(2):
            remote(ref, ref, *ring_sems(u, 0, way), a_devices[way]).start()

    def wait_ring(u, stage):
        for way in range(2):
            ref = line_y(u, 0, 64 * way if stage == 3 else None) if stage >= 2 else block(u, 0, 64 * way if stage == 1 else None)
            wait_for(ref, ring_recv.at[u, stage, way])

    def a2(u):
        wait_ring(u, 0)
        for way in range(2):
            ref = block(u, chip_at(a_prev if way == 0 else a_next, across), 64 * way)
            remote(ref, ref, *ring_sems(u, 1, way), a_devices[way]).start()

    def b_send(u, stage, spots, halves):
        @pl.when(core == 0)
        def _():
            for way in range(2):
                ref = line_x(u, spots[way], 64 * way if halves else None)
                remote(ref, ref, *ring_sems(u, stage, way), b_devices[way]).start()

        @pl.when(core == 1)
        def _():
            for way in range(2):
                ref = line_y(u, spots[way], 64 * way if halves else None)
                remote(ref, ref, *ring_sems(u, stage, way), b_devices[way]).start()

    def b1(u):
        if u < DIRECT:
            wait_ring(u, 0)
            wait_for(block(u, 0), ring_recv.at[u, 1, 0])
        else:
            wait_ring(u, 1)
        b_send(u, 2, (across, across), False)

    def b2(u):
        wait_ring(u, 2)
        b_send(u, 3, (b_prev, b_next), True)

    def b_done(u):
        wait_ring(u, 3)

    def ring_wait_sends(u):
        for stage in range(4):
            if u < DIRECT and stage == 1:
                wait_for(block(u, 0), ring_send.at[u, 1, 0])
                continue
            for way in range(2):
                half = 64 * way if stage in (1, 3) else None
                ref = line_y(u, 0, half) if stage >= 2 else block(u, 0, half)
                wait_for(ref, ring_send.at[u, stage, way])

    partner = column_dev(core, z + 1 - 2 * member)
    sibling = column_dev(1 - core, z)

    def token_rows(c, m, i):
        return x_all.at[c, m, pl.ds(i * PART, PART)]

    def normalize(i):
        for copy in in_copies(i):
            copy.wait()

        def rows16(j, carry):
            rows = pl.ds(pl.multiple_of(i * PART + j * 16, 16), 16)
            values = tok[rows, :].astype(F32)
            center = values - jnp.mean(values, axis=-1, keepdims=True)
            spread = jnp.mean(center * center, axis=-1, keepdims=True)
            scaled = center * lax.rsqrt(spread + 1e-05) * gain[...] + bias[...]
            x_all[core, member, rows, :] = (scaled * (mask[rows, :].astype(F32) * (1.0 / 0.9))).astype(BF16)
            return carry

        lax.fori_loop(0, PART // 16, rows16, 0)

    def send_tokens(i):
        ref = token_rows(core, member, i)
        remote(ref, ref, tok_send.at[0, i], tok_recv.at[i], partner).start()
        remote(ref, ref, tok_send.at[1, i], sib_recv.at[0, i], sibling).start()

    def forward_tokens(i):
        ref = token_rows(core, 1 - member, i)
        wait_for(ref, tok_recv.at[i])
        remote(ref, ref, fwd_send.at[i], sib_recv.at[1, i], sibling).start()

    def project(s, w, m):
        weights = w_all.at[s, w]

        def rows256(c, carry):
            product = jnp.dot(x_all[c, m], weights[...].reshape(D, 256), preferred_element_type=F32)
            rows = pl.ds(pl.multiple_of(m * OWN, OWN), OWN)
            qkv[s, w, c, rows, :] = product.astype(BF16)
            return carry

        lax.fori_loop(0, 2, rows256, 0)

    def start_of(position):
        first = jnp.full_like(position, -1)
        for i in range(8):
            first = jnp.where(traj[i] <= position, traj[i], first)
        return first

    def keeps(first, length):
        return jnp.where(start_of(first + (length - 1)) < first, 1.0, 0.0).astype(F32)

    chip_first = chip * 8 * SPAN

    keep_spans = []

    def span_first(c):
        return chip_first + (c * 4 + pair) * SPAN

    def states(s):
        def one_span(c, carry):
            first = span_first(c)
            last_start = start_of(first + (SPAN - 1))
            spots = first + lax.broadcasted_iota(I32, (SPAN, HEAD), 0)
            kept = spots >= last_start
            for h in range(2):
                columns = slice(h * HEAD, (h + 1) * HEAD)
                values = jnp.where(kept, qkv[s, 2, c, :, columns].astype(F32), 0.0).astype(BF16)
                state = lax.dot_general(
                    qkv[s, 1, c, :, columns], values, (((0,), (0,)), ((), ())), preferred_element_type=F32
                )
                a_out[s, c, columns, :] = state.astype(BF16)
            return carry

        lax.fori_loop(0, 2, one_span, 0)

    def send_states(s):
        mine = dists[s]
        for i in range(1, 4):
            other = (mine + i) % 4
            remote(
                a_out.at[s, :, pl.ds(pl.multiple_of(other * 64, 64), 64)], rz.at[slot_of(other), :, pair],
                rz_send.at[s, i - 1], rz_recv.at[slot_of(other), pair],
                column_dev(core_of(other), plane_at(planes[s], other)),
            ).start()
        rz[s, :, pair] = a_out[s, :, pl.ds(pl.multiple_of(mine * 64, 64), 64), :]

    def wait_states(s):
        for i in range(1, 4):
            spot = (pair + i) % 4
            wait_for(rz.at[s, :, spot], rz_recv.at[s, spot])

    half = chip // 8
    eighth = chip % 8

    def chip_totals(s):
        total = jnp.zeros((64, HEAD), F32)
        for j in range(8):
            local_c[s, j // 4, j % 4] = total.astype(BF16)
            total = total * keep_spans[j] + rz[s, j // 4, j % 4].astype(F32)
        t_all[s] = total

        def send(i, carry):
            other = (chip + i) % 16
            remote(
                t_all.at[s, pl.ds(pl.multiple_of((other % 8) * 8, 8), 8)], tp.at[s, chip], a2a_send.at[s], a2a_recv.at[s],
                plane_dev(other),
            ).start()
            return carry

        lax.fori_loop(1, 16, send, 0)
        tp[s, chip] = t_all[s, pl.ds(pl.multiple_of(eighth * 8, 8), 8), :]

    def send_local(s):
        mine = dists[s]
        rows = pl.ds(pl.multiple_of(mine * 64, 64), 64)
        for i in range(1, 4):
            other = (mine + i) % 4
            plane = plane_at(planes[s], other)
            remote(
                local_c.at[s, :, plane // 2], local_in.at[slot_of(other), :, rows],
                local_send.at[s, i - 1], local_recv.at[slot_of(other), mine],
                column_dev(core_of(other), plane),
            ).start()
        local_in[s, :, rows, :] = local_c[s, :, pair]

    def prefixes(s):
        wait_for(tp.at[s, pl.ds(0, 15)], a2a_recv.at[s])
        total = jnp.zeros((8, HEAD), F32)
        for k in range(16):
            ps[s, k] = total
            if k < 15:
                total = total * keeps(k * 8 * SPAN, 8 * SPAN) + tp[s, k]
        mine = dists[s]
        spot = mine * 8 + eighth
        targets = []
        for near in range(4):
            dist = (mine + near) % 4
            targets.append((core_of(dist), plane_at(planes[s], dist), prefix_in.at[slot_of(dist), spot], slot_of(dist)))

        def to_chip(i, carry):
            other = half * 8 + (eighth + i) % 8
            for near, (core_id, plane, dst, slot) in enumerate(targets):
                copy = remote(ps.at[s, other], dst, prefix_send.at[s], prefix_recv.at[slot], (other * 2 + core_id, plane))
                if near == 0:
                    pl.when(i != 0)(copy.start)
                else:
                    copy.start()
            return carry

        lax.fori_loop(0, 8, to_chip, 0)
        prefix_in[s, spot] = ps[s, chip]

    def wait_prefix(s):
        wait_for(prefix_in.at[s, pl.ds(0, 31)], prefix_recv.at[s])

    def wait_local(s):
        for i in range(1, 4):
            spot = (dists[s] + i) % 4
            wait_for(local_in.at[s, :, pl.ds(0, 64)], local_recv.at[s, spot])

    def inside_terms(s):
        def one_span(c, carry):
            first = span_first(c)
            for top in (0, 256):
                span_keys = top + 256
                rows = first + top + lax.broadcasted_iota(I32, (256, 1), 0)
                spots = first + lax.broadcasted_iota(I32, (256, span_keys), 1)
                allowed = (spots <= rows) & (spots >= start_of(rows))
                for h in range(2):
                    columns = slice(h * HEAD, (h + 1) * HEAD)
                    scores = lax.dot_general(
                        qkv[s, 0, c, top:top + 256, columns], qkv[s, 1, c, :span_keys, columns],
                        (((1,), (1,)), ((), ())), preferred_element_type=F32,
                    )
                    rounded = jnp.where(allowed, scores, 0.0).astype(BF16)
                    inside[s, c, top:top + 256, columns] = jnp.dot(
                        rounded, qkv[s, 2, c, :span_keys, columns], preferred_element_type=F32
                    )
            return carry

        lax.fori_loop(0, 2, one_span, 0)

    def finish(s, c):
        first = span_first(c)
        reach = jnp.ones((), F32)
        for j in range(7):
            reach = jnp.where(j < c * 4 + pair, reach * keep_spans[j], reach)
        for top in (0, 256):
            rows = first + top + lax.broadcasted_iota(I32, (256, 1), 0)
            reached = start_of(rows) < first
            for h in range(2):
                columns = slice(h * HEAD, (h + 1) * HEAD)
                queries = qkv[s, 0, c, top:top + 256, columns]
                prefix = prefix_in[s, h * 16:(h + 1) * 16].reshape(HEAD, HEAD)
                state = local_in[s, c, columns, :].astype(F32) + prefix * reach
                high = state.astype(BF16)
                low = (state - high.astype(F32)).astype(BF16)
                term = jnp.dot(queries, high, preferred_element_type=F32)
                term += jnp.dot(queries, low, preferred_element_type=F32)
                mixed = inside[s, c, top:top + 256, columns] + jnp.where(reached, term, 0.0)
                scale_back = lax.rsqrt(jnp.mean(mixed * mixed, axis=-1, keepdims=True) + 1e-06)
                outs[s, c, top:top + 256, columns] = (mixed * scale_back * gains[s, :, columns]).astype(BF16)

    def send_out(s, c):
        rows = pl.ds(pl.multiple_of(pair * SPAN, SPAN), SPAN)
        device = column_dev(c, planes[s])
        args = (outs.at[s, c], out.at[rows])
        if s == 1 and c == 0:

            @pl.when(core == 0)
            def _():
                pltpu.make_async_copy(*args, out_recv.at[pair]).start()

            @pl.when(core == 1)
            def _():
                remote(*args, out_send.at[s, c], out_recv.at[pair], device).start()

        else:
            remote(*args, out_send.at[s, c], out_recv.at[pair], device).start()

    for copy in small_copies:
        copy.wait()
    normalize(0)
    pl.semaphore_wait(barrier, 30)
    send_tokens(0)
    send_weights(KEY, (0, 1))
    send_weights(KEY, (3, 2))
    send_weights(VALUE, (3, 2))
    send_weights(VALUE, (0, 1))
    normalize(1)
    send_tokens(1)
    normalize(2)
    send_tokens(2)
    a_direct(0)
    normalize(3)
    send_tokens(3)
    a1(1)
    b1(0)
    a1(2)
    send_weights(QUERY, (3, 2, 1, 0))
    send_gains()
    forward_tokens(0)
    keep_spans.extend(keeps(chip_first + j * SPAN, SPAN) for j in range(8))
    a2(1)
    a2(2)
    a1(3)
    b2(0)
    b1(1)
    forward_tokens(1)
    b1(2)
    a2(3)
    for i in range(PARTS):
        wait_for(token_rows(1 - core, member, i), sib_recv.at[0, i])
    b_done(0)
    project(1, KEY, member)
    b2(1)
    forward_tokens(2)
    b1(3)
    b2(2)
    b_done(1)
    project(0, KEY, member)
    forward_tokens(3)
    b_done(2)
    b2(3)
    a1(4)
    a1(5)
    project(0, VALUE, member)
    for i in range(PARTS):
        wait_for(token_rows(1 - core, 1 - member, i), sib_recv.at[1, i])
    project(0, KEY, 1 - member)
    project(0, VALUE, 1 - member)
    states(0)
    send_states(0)
    a2(4)
    a2(5)
    project(1, KEY, 1 - member)
    b1(4)
    b1(5)
    b_done(3)
    project(1, VALUE, member)
    project(1, VALUE, 1 - member)
    states(1)
    send_states(1)
    wait_states(0)
    chip_totals(0)
    send_local(0)
    b2(4)
    prefixes(0)
    wait_states(1)
    chip_totals(1)
    send_local(1)
    b2(5)
    b_done(4)
    for m in range(2):
        project(0, QUERY, m)
    inside_terms(0)
    prefixes(1)

    @pl.when(core == 0)
    def _():
        wait_for(gains.at[0], hg_recv.at[0])
        wait_for(gains.at[1], small_sem.at[3])

    @pl.when(core == 1)
    def _():
        for s in range(2):
            wait_for(gains.at[s], hg_recv.at[s])

    wait_local(0)
    wait_prefix(0)
    for c in range(2):
        finish(0, c)
        send_out(0, c)
    b_done(5)
    for m in range(2):
        project(1, QUERY, m)
    inside_terms(1)
    wait_local(1)
    wait_prefix(1)
    for c in range(2):
        finish(1, c)
        send_out(1, c)

    ref = w_all.at[0, 0, 0, 0, pl.ds(0, 64)]
    for w in range(3):
        for d in (1, 2, 3):
            wait_for(ref, wz_send.at[d, w])

    @pl.when(core == 1)
    def _():
        for w in range(3):
            wait_for(ref, wz_send.at[0, w])

    @pl.when(core == 0)
    def _():
        wait_for(gains.at[0], hg_send.at[0])

    @pl.when(core == 1)
    def _():
        for s in range(2):
            wait_for(gains.at[s], hg_send.at[s])

    for u in range(len(UNITS)):
        ring_wait_sends(u)
    for i in range(PARTS):
        ref = token_rows(0, 0, i)
        for sem in (tok_send.at[0, i], tok_send.at[1, i], fwd_send.at[i]):
            wait_for(ref, sem)
    for s in range(2):
        for i in range(3):
            wait_for(rz.at[s, :, 0], rz_send.at[s, i])
            wait_for(local_c.at[s, :, 0], local_send.at[s, i])
    for s in range(2):
        wait_for(tp.at[s, pl.ds(0, 15)], a2a_send.at[s])
        wait_for(prefix_in.at[s, pl.ds(0, 31)], prefix_send.at[s])
    for s in range(2):
        for c in range(2):
            if s == 1 and c == 0:

                @pl.when(core == 1)
                def _():
                    wait_for(outs.at[s, c], out_send.at[s, c])

            else:
                wait_for(outs.at[s, c], out_send.at[s, c])
    for p in range(4):
        wait_for(outs.at[0, 0], out_recv.at[p])


def per_device(tokens, norm_gain, norm_bias, keep_mask, projection, head_gain, traj_starts):
    any_spec = pl.BlockSpec(memory_space=pl.ANY)
    dma = pltpu.SemaphoreType.DMA
    return pl.pallas_call(
        kernel,
        out_shape=jax.ShapeDtypeStruct((2048, 256), BF16),
        in_specs=[any_spec] * 7,
        out_specs=any_spec,
        scratch_shapes=[
            pltpu.VMEM((1, D), F32),
            pltpu.VMEM((1, D), F32),
            pltpu.SMEM((8,), I32),
            pltpu.VMEM((OWN, D), BF16),
            pltpu.VMEM((OWN, D), I32),
            pltpu.VMEM((2, 2, OWN, D), BF16),
            pltpu.VMEM((2, 3, 4, 4, 128, 256), BF16),
            pltpu.VMEM((2, 3, 2, SPAN, 256), BF16),
            pltpu.VMEM((2, 2, SPAN, 256), F32),
            pltpu.VMEM((2, 2, 256, HEAD), BF16),
            pltpu.VMEM((2, 2, 4, 64, HEAD), BF16),
            pltpu.VMEM((2, 2, 4, 64, HEAD), BF16),
            pltpu.VMEM((2, 64, HEAD), F32),
            pltpu.VMEM((2, 16, 8, HEAD), F32),
            pltpu.VMEM((2, 16, 8, HEAD), F32),
            pltpu.VMEM((2, 2, 256, HEAD), BF16),
            pltpu.VMEM((2, 32, 8, HEAD), F32),
            pltpu.VMEM((2, 1, 256), F32),
            pltpu.VMEM((2, 2, SPAN, 256), BF16),
            dma((2, PARTS)),
            dma((4,)),
            dma((4, 3)),
            dma((2, 3, 2)),
            dma((len(UNITS), 4, 2)),
            dma((len(UNITS), 4, 2)),
            dma((2, PARTS)),
            dma((PARTS,)),
            dma((PARTS,)),
            dma((2, PARTS)),
            dma((2,)),
            dma((2,)),
            dma((2, 3)),
            dma((2, 4)),
            dma((2,)),
            dma((2,)),
            dma((2, 3)),
            dma((2, 4)),
            dma((2,)),
            dma((2,)),
            dma((2, 2)),
            dma((4,)),
        ],
        compiler_params=pltpu.CompilerParams(
            collective_id=0, has_side_effects=True, vmem_limit_bytes=63 * 1024 * 1024
        ),
    )(
        tokens, norm_gain.reshape(1, D), norm_bias.reshape(1, D), keep_mask, projection,
        head_gain.reshape(1, 256), traj_starts,
    )


def solution(mesh):
    placed = (
        P(("outer", "inner"), None),
        P(),
        P(),
        P(("outer", "inner"), None),
        P(None, "outer", "inner"),
        P("inner"),
        P(),
    )
    return jax.shard_map(
        per_device, mesh=mesh, in_specs=placed, out_specs=P("outer", "inner"), check_vma=False
    )
```

```python
import jax
import jax.numpy as jnp
from jax import lax
from jax.experimental import pallas as pl
from jax.experimental.pallas import tpu as pltpu
from jax.sharding import PartitionSpec as P

MESH = pl.DeviceIdType.MESH
F32, BF16, I32 = jnp.float32, jnp.bfloat16, jnp.int32
D, HEAD, SPAN = 2048, 128, 512
OWN = 256
DIRECT = 1
PARTS = 4
PART = OWN // PARTS
QUERY, KEY, VALUE = 0, 1, 2
UNITS = ((1, KEY), (0, KEY), (0, VALUE), (1, VALUE), (0, QUERY), (1, QUERY))


def core_of(dist):
    return ((dist + 1) // 2) % 2


def plane_at(head_plane, dist):
    up = (head_plane + dist) % 8
    down = (head_plane + 8 - dist) % 8
    return jnp.where(up % 2 == 0, up, down)


def kernel(
    tok_hbm, gain_hbm, bias_hbm, mask_hbm, proj_hbm, head_gain, traj_hbm, out,
    gain, bias, traj, tok, mask, x_all, w_all, qkv, inside, a_out, rz, local_c, t_all, tp, ps, local_in, prefix_in, gains, outs,
    in_sem, small_sem, wz_send, wz_recv, ring_send, ring_recv, tok_send, tok_recv, fwd_send, sib_recv, hg_send, hg_recv,
    rz_send, rz_recv, a2a_send, a2a_recv, local_send, local_recv, prefix_send, prefix_recv, out_send, out_recv,
):
    outer, z = lax.axis_index("outer"), lax.axis_index("inner")
    core, chip = outer % 2, outer // 2
    cx, cy = chip // 4, chip % 4
    pair, member = z // 2, z % 2
    along = jnp.where(core == 0, cx, cy)
    across = jnp.where(core == 0, cy, cx)

    def chip_at(a, b):
        return a * (4 - 3 * core) + b * (1 + 3 * core)

    a_next, a_prev = (along + 1) % 4, (along + 3) % 4
    b_next, b_prev = (across + 1) % 4, (across + 3) % 4

    def plane_dev(chip_id):
        return (chip_id * 2 + core, z)

    def column_dev(core_id, plane):
        return (chip * 2 + core_id, plane)

    dists = tuple(jnp.where((z + s) % 2 == 0, 2 * core, 3 - 2 * core) for s in range(2))
    own_slot = z % 2
    step = 2 * member - 1
    planes = tuple((z + step * d + 8) % 8 for d in dists)

    def remote(src, dst, send, recv, device):
        return pltpu.make_async_remote_copy(
            src_ref=src, dst_ref=dst, send_sem=send, recv_sem=recv, device_id=device, device_id_type=MESH
        )

    def wait_for(ref, sem):
        pltpu.make_async_copy(ref, ref, sem).wait()

    def in_copies(i):
        rows = pl.ds(i * PART, PART)
        return (
            pltpu.make_async_copy(tok_hbm.at[rows], tok.at[rows], in_sem.at[0, i]),
            pltpu.make_async_copy(mask_hbm.at[rows], mask.at[rows], in_sem.at[1, i]),
        )

    small_copies = (
        pltpu.make_async_copy(gain_hbm, gain, small_sem.at[0]),
        pltpu.make_async_copy(bias_hbm, bias, small_sem.at[1]),
        pltpu.make_async_copy(traj_hbm, traj, small_sem.at[2]),
    )
    for copy in in_copies(0) + small_copies:
        copy.start()
    for i in range(1, PARTS):
        for copy in in_copies(i):
            copy.start()

    barrier = pltpu.get_barrier_semaphore()

    def greet_plane(i, carry):
        pl.semaphore_signal(barrier, inc=1, device_id=plane_dev((chip + i) % 16), device_id_type=MESH)
        return carry

    def greet_column(i, carry):
        spot = (z * 2 + core + i) % 16
        pl.semaphore_signal(barrier, inc=1, device_id=column_dev(spot % 2, spot // 2), device_id_type=MESH)
        return carry

    lax.fori_loop(1, 16, greet_column, 0)
    lax.fori_loop(1, 16, greet_plane, 0)

    def wz_copy(d, w):
        src = proj_hbm.at[w]
        dst = w_all.at[own_slot, w, cx, cy, pl.ds(core * 64, 64)]
        return src, dst, wz_send.at[d, w], wz_recv.at[own_slot, w, core], column_dev(core_of(d), plane_at(z, d))

    def send_weights(w, which):
        for d in which:
            src, dst, send, recv, device = wz_copy(d, w)
            if d == 0:

                @pl.when(core == 0)
                def _():
                    pltpu.make_async_copy(src, dst, recv).start()

                @pl.when(core == 1)
                def _():
                    remote(src, dst, send, recv, device).start()

            else:
                remote(src, dst, send, recv, device).start()

    def send_gains():
        for d in (1, 2, 3):

            @pl.when(core == core_of(d))
            def _():
                remote(
                    head_gain, gains.at[own_slot], hg_send.at[d - 1], hg_recv.at[own_slot], column_dev(core, plane_at(z, d))
                ).start()

        @pl.when(core == 0)
        def _():
            pltpu.make_async_copy(head_gain, gains.at[own_slot], small_sem.at[3]).start()

    def wait_wz(u):
        s, w = UNITS[u]
        for half in range(2):
            wait_for(w_all.at[s, w, 0, 0, pl.ds(half * 64, 64)], wz_recv.at[s, w, half])

    def block(u, chip_id, rows=None):
        ref = w_all.at[(*UNITS[u], chip_id // 4, chip_id % 4)]
        return ref if rows is None else ref.at[pl.ds(rows, 64)]

    def line_x(u, b, rows=None):
        ref = w_all.at[(*UNITS[u], slice(None), b)]
        return ref if rows is None else ref.at[:, pl.ds(rows, 64)]

    def line_y(u, b, rows=None):
        ref = w_all.at[(*UNITS[u], b)]
        return ref if rows is None else ref.at[:, pl.ds(rows, 64)]

    def ring_sems(u, stage, way):
        return ring_send.at[u, stage, way], ring_recv.at[u, stage, way]

    a_devices = (plane_dev(chip_at(a_next, across)), plane_dev(chip_at(a_prev, across)))
    b_devices = (plane_dev(chip_at(along, b_next)), plane_dev(chip_at(along, b_prev)))

    def a1(u):
        wait_wz(u)
        for way in range(2):
            ref = block(u, chip)
            remote(ref, ref, *ring_sems(u, 0, way), a_devices[way]).start()

    def a_direct(u):
        wait_wz(u)
        ref = block(u, chip)
        remote(ref, ref, *ring_sems(u, 1, 0), plane_dev(chip_at((along + 2) % 4, across))).start()
        for way in range(2):
            remote(ref, ref, *ring_sems(u, 0, way), a_devices[way]).start()

    def wait_ring(u, stage):
        for way in range(2):
            ref = line_y(u, 0, 64 * way if stage == 3 else None) if stage >= 2 else block(u, 0, 64 * way if stage == 1 else None)
            wait_for(ref, ring_recv.at[u, stage, way])

    def a2(u):
        wait_ring(u, 0)
        for way in range(2):
            ref = block(u, chip_at(a_prev if way == 0 else a_next, across), 64 * way)
            remote(ref, ref, *ring_sems(u, 1, way), a_devices[way]).start()

    def b_send(u, stage, spots, halves):
        @pl.when(core == 0)
        def _():
            for way in range(2):
                ref = line_x(u, spots[way], 64 * way if halves else None)
                remote(ref, ref, *ring_sems(u, stage, way), b_devices[way]).start()

        @pl.when(core == 1)
        def _():
            for way in range(2):
                ref = line_y(u, spots[way], 64 * way if halves else None)
                remote(ref, ref, *ring_sems(u, stage, way), b_devices[way]).start()

    def b1(u):
        if u < DIRECT:
            wait_ring(u, 0)
            wait_for(block(u, 0), ring_recv.at[u, 1, 0])
        else:
            wait_ring(u, 1)
        b_send(u, 2, (across, across), False)

    def b2(u):
        wait_ring(u, 2)
        b_send(u, 3, (b_prev, b_next), True)

    def b_done(u):
        wait_ring(u, 3)

    def ring_wait_sends(u):
        for stage in range(4):
            if u < DIRECT and stage == 1:
                wait_for(block(u, 0), ring_send.at[u, 1, 0])
                continue
            for way in range(2):
                half = 64 * way if stage in (1, 3) else None
                ref = line_y(u, 0, half) if stage >= 2 else block(u, 0, half)
                wait_for(ref, ring_send.at[u, stage, way])

    partner = column_dev(core, z + 1 - 2 * member)
    sibling = column_dev(1 - core, z)

    def token_rows(c, m, i):
        return x_all.at[c, m, pl.ds(i * PART, PART)]

    def normalize(i):
        for copy in in_copies(i):
            copy.wait()

        def rows16(j, carry):
            rows = pl.ds(pl.multiple_of(i * PART + j * 16, 16), 16)
            values = tok[rows, :].astype(F32)
            center = values - jnp.mean(values, axis=-1, keepdims=True)
            spread = jnp.mean(center * center, axis=-1, keepdims=True)
            scaled = center * lax.rsqrt(spread + 1e-05) * gain[...] + bias[...]
            x_all[core, member, rows, :] = (scaled * (mask[rows, :].astype(F32) * (1.0 / 0.9))).astype(BF16)
            return carry

        lax.fori_loop(0, PART // 16, rows16, 0)

    def send_tokens(i):
        ref = token_rows(core, member, i)
        remote(ref, ref, tok_send.at[0, i], tok_recv.at[i], partner).start()
        remote(ref, ref, tok_send.at[1, i], sib_recv.at[0, i], sibling).start()

    def forward_tokens(i):
        ref = token_rows(core, 1 - member, i)
        wait_for(ref, tok_recv.at[i])
        remote(ref, ref, fwd_send.at[i], sib_recv.at[1, i], sibling).start()

    def project(s, w, m):
        weights = w_all.at[s, w]

        def rows256(c, carry):
            product = jnp.dot(x_all[c, m], weights[...].reshape(D, 256), preferred_element_type=F32)
            rows = pl.ds(pl.multiple_of(m * OWN, OWN), OWN)
            qkv[s, w, c, rows, :] = product.astype(BF16)
            return carry

        lax.fori_loop(0, 2, rows256, 0)

    def start_of(position):
        first = jnp.full_like(position, -1)
        for i in range(8):
            first = jnp.where(traj[i] <= position, traj[i], first)
        return first

    def keeps(first, length):
        return jnp.where(start_of(first + (length - 1)) < first, 1.0, 0.0).astype(F32)

    chip_first = chip * 8 * SPAN

    keep_spans = []

    def span_first(c):
        return chip_first + (c * 4 + pair) * SPAN

    def states(s):
        def one_span(c, carry):
            first = span_first(c)
            last_start = start_of(first + (SPAN - 1))
            spots = first + lax.broadcasted_iota(I32, (SPAN, HEAD), 0)
            kept = spots >= last_start
            for h in range(2):
                columns = slice(h * HEAD, (h + 1) * HEAD)
                values = jnp.where(kept, qkv[s, 2, c, :, columns].astype(F32), 0.0).astype(BF16)
                state = lax.dot_general(
                    qkv[s, 1, c, :, columns], values, (((0,), (0,)), ((), ())), preferred_element_type=F32
                )
                a_out[s, c, columns, :] = state.astype(BF16)
            return carry

        lax.fori_loop(0, 2, one_span, 0)

    def send_states(s):
        mine = dists[s]
        for i in range(1, 4):
            other = (mine + i) % 4
            remote(
                a_out.at[s, :, pl.ds(pl.multiple_of(other * 64, 64), 64)], rz.at[s, :, pair],
                rz_send.at[s, i - 1], rz_recv.at[s, pair],
                column_dev(core_of(other), plane_at(planes[s], other)),
            ).start()
        rz[s, :, pair] = a_out[s, :, pl.ds(pl.multiple_of(mine * 64, 64), 64), :]

    def wait_states(s):
        for i in range(1, 4):
            spot = (pair + i) % 4
            wait_for(rz.at[s, :, spot], rz_recv.at[s, spot])

    half = chip // 8
    eighth = chip % 8

    def chip_totals(s):
        total = jnp.zeros((64, HEAD), F32)
        for j in range(8):
            local_c[s, j // 4, j % 4] = total.astype(BF16)
            total = total * keep_spans[j] + rz[s, j // 4, j % 4].astype(F32)
        t_all[s] = total

        def send(i, carry):
            other = (chip + i) % 16
            remote(
                t_all.at[s, pl.ds(pl.multiple_of((other % 8) * 8, 8), 8)], tp.at[s, chip], a2a_send.at[s], a2a_recv.at[s],
                plane_dev(other),
            ).start()
            return carry

        lax.fori_loop(1, 16, send, 0)
        tp[s, chip] = t_all[s, pl.ds(pl.multiple_of(eighth * 8, 8), 8), :]

    def send_local(s):
        mine = dists[s]
        rows = pl.ds(pl.multiple_of(mine * 64, 64), 64)
        for i in range(1, 4):
            other = (mine + i) % 4
            plane = plane_at(planes[s], other)
            remote(
                local_c.at[s, :, plane // 2], local_in.at[s, :, rows],
                local_send.at[s, i - 1], local_recv.at[s, mine],
                column_dev(core_of(other), plane),
            ).start()
        local_in[s, :, rows, :] = local_c[s, :, pair]

    def prefixes(s):
        wait_for(tp.at[s, pl.ds(0, 15)], a2a_recv.at[s])
        total = jnp.zeros((8, HEAD), F32)
        for k in range(16):
            ps[s, k] = total
            if k < 15:
                total = total * keeps(k * 8 * SPAN, 8 * SPAN) + tp[s, k]
        mine = dists[s]
        spot = mine * 8 + eighth
        targets = []
        for near in range(4):
            dist = (mine + near) % 4
            targets.append((core_of(dist), plane_at(planes[s], dist), prefix_in.at[s, spot]))

        def to_chip(i, carry):
            other = half * 8 + (eighth + i) % 8
            for near, (core_id, plane, dst) in enumerate(targets):
                copy = remote(ps.at[s, other], dst, prefix_send.at[s], prefix_recv.at[s], (other * 2 + core_id, plane))
                if near == 0:
                    pl.when(i != 0)(copy.start)
                else:
                    copy.start()
            return carry

        lax.fori_loop(0, 8, to_chip, 0)
        prefix_in[s, spot] = ps[s, chip]

    def wait_prefix(s):
        wait_for(prefix_in.at[s, pl.ds(0, 31)], prefix_recv.at[s])

    def wait_local(s):
        for i in range(1, 4):
            spot = (dists[s] + i) % 4
            wait_for(local_in.at[s, :, pl.ds(0, 64)], local_recv.at[s, spot])

    def inside_terms(s):
        def one_span(c, carry):
            first = span_first(c)
            for top in (0, 256):
                span_keys = top + 256
                rows = first + top + lax.broadcasted_iota(I32, (256, 1), 0)
                spots = first + lax.broadcasted_iota(I32, (256, span_keys), 1)
                allowed = (spots <= rows) & (spots >= start_of(rows))
                for h in range(2):
                    columns = slice(h * HEAD, (h + 1) * HEAD)
                    scores = lax.dot_general(
                        qkv[s, 0, c, top:top + 256, columns], qkv[s, 1, c, :span_keys, columns],
                        (((1,), (1,)), ((), ())), preferred_element_type=F32,
                    )
                    rounded = jnp.where(allowed, scores, 0.0).astype(BF16)
                    inside[s, c, top:top + 256, columns] = jnp.dot(
                        rounded, qkv[s, 2, c, :span_keys, columns], preferred_element_type=F32
                    )
            return carry

        lax.fori_loop(0, 2, one_span, 0)

    def finish(s, c):
        first = span_first(c)
        reach = jnp.ones((), F32)
        for j in range(7):
            reach = jnp.where(j < c * 4 + pair, reach * keep_spans[j], reach)
        for top in (0, 256):
            rows = first + top + lax.broadcasted_iota(I32, (256, 1), 0)
            reached = start_of(rows) < first
            for h in range(2):
                columns = slice(h * HEAD, (h + 1) * HEAD)
                queries = qkv[s, 0, c, top:top + 256, columns]
                prefix = prefix_in[s, h * 16:(h + 1) * 16].reshape(HEAD, HEAD)
                state = local_in[s, c, columns, :].astype(F32) + prefix * reach
                high = state.astype(BF16)
                low = (state - high.astype(F32)).astype(BF16)
                term = jnp.dot(queries, high, preferred_element_type=F32)
                term += jnp.dot(queries, low, preferred_element_type=F32)
                mixed = inside[s, c, top:top + 256, columns] + jnp.where(reached, term, 0.0)
                scale_back = lax.rsqrt(jnp.mean(mixed * mixed, axis=-1, keepdims=True) + 1e-06)
                outs[s, c, top:top + 256, columns] = (mixed * scale_back * gains[s, :, columns]).astype(BF16)

    def send_out(s, c):
        rows = pl.ds(pl.multiple_of(pair * SPAN, SPAN), SPAN)
        device = column_dev(c, planes[s])
        args = (outs.at[s, c], out.at[rows])
        if c == 0:

            @pl.when(dists[s] == 0)
            def _():
                pltpu.make_async_copy(*args, out_recv.at[pair]).start()

            @pl.when(dists[s] != 0)
            def _():
                remote(*args, out_send.at[s, c], out_recv.at[pair], device).start()

        else:
            remote(*args, out_send.at[s, c], out_recv.at[pair], device).start()

    for copy in small_copies:
        copy.wait()
    normalize(0)
    pl.semaphore_wait(barrier, 30)
    send_tokens(0)
    send_weights(KEY, (0, 1, 2, 3))
    send_weights(VALUE, (0, 1, 2, 3))
    normalize(1)
    send_tokens(1)
    normalize(2)
    send_tokens(2)
    a_direct(0)
    normalize(3)
    send_tokens(3)
    a1(1)
    b1(0)
    a1(2)
    send_weights(QUERY, (3, 2, 1, 0))
    send_gains()
    forward_tokens(0)
    keep_spans.extend(keeps(chip_first + j * SPAN, SPAN) for j in range(8))
    a2(1)
    a2(2)
    a1(3)
    b2(0)
    b1(1)
    forward_tokens(1)
    b1(2)
    a2(3)
    for i in range(PARTS):
        wait_for(token_rows(1 - core, member, i), sib_recv.at[0, i])
    b_done(0)
    project(1, KEY, member)
    b2(1)
    forward_tokens(2)
    b1(3)
    b2(2)
    b_done(1)
    project(0, KEY, member)
    forward_tokens(3)
    b_done(2)
    b2(3)
    a1(4)
    a1(5)
    project(0, VALUE, member)
    for i in range(PARTS):
        wait_for(token_rows(1 - core, 1 - member, i), sib_recv.at[1, i])
    project(0, KEY, 1 - member)
    project(0, VALUE, 1 - member)
    states(0)
    send_states(0)
    a2(4)
    a2(5)
    project(1, KEY, 1 - member)
    b1(4)
    b1(5)
    b_done(3)
    project(1, VALUE, member)
    project(1, VALUE, 1 - member)
    states(1)
    send_states(1)
    wait_states(0)
    chip_totals(0)
    send_local(0)
    b2(4)
    prefixes(0)
    wait_states(1)
    chip_totals(1)
    send_local(1)
    b2(5)
    b_done(4)
    for m in range(2):
        project(0, QUERY, m)
    inside_terms(0)
    prefixes(1)

    @pl.when(core == 0)
    def _():
        wait_for(gains.at[0], hg_recv.at[1 - own_slot])
        wait_for(gains.at[0], small_sem.at[3])

    @pl.when(core == 1)
    def _():
        for s in range(2):
            wait_for(gains.at[s], hg_recv.at[s])

    wait_local(0)
    wait_prefix(0)
    for c in range(2):
        finish(0, c)
        send_out(0, c)
    b_done(5)
    for m in range(2):
        project(1, QUERY, m)
    inside_terms(1)
    wait_local(1)
    wait_prefix(1)
    for c in range(2):
        finish(1, c)
        send_out(1, c)

    ref = w_all.at[0, 0, 0, 0, pl.ds(0, 64)]
    for w in range(3):
        for d in (1, 2, 3):
            wait_for(ref, wz_send.at[d, w])

    @pl.when(core == 1)
    def _():
        for w in range(3):
            wait_for(ref, wz_send.at[0, w])

    @pl.when(core == 0)
    def _():
        wait_for(gains.at[0], hg_send.at[2])

    @pl.when(core == 1)
    def _():
        for i in range(2):
            wait_for(gains.at[0], hg_send.at[i])

    for u in range(len(UNITS)):
        ring_wait_sends(u)
    for i in range(PARTS):
        ref = token_rows(0, 0, i)
        for sem in (tok_send.at[0, i], tok_send.at[1, i], fwd_send.at[i]):
            wait_for(ref, sem)
    for s in range(2):
        for i in range(3):
            wait_for(rz.at[s, :, 0], rz_send.at[s, i])
            wait_for(local_c.at[s, :, 0], local_send.at[s, i])
    for s in range(2):
        wait_for(tp.at[s, pl.ds(0, 15)], a2a_send.at[s])
        wait_for(prefix_in.at[s, pl.ds(0, 31)], prefix_send.at[s])
    for s in range(2):
        for c in range(2):
            if c == 0:

                @pl.when(dists[s] != 0)
                def _():
                    wait_for(outs.at[s, c], out_send.at[s, c])

            else:
                wait_for(outs.at[s, c], out_send.at[s, c])
    for p in range(4):
        wait_for(outs.at[0, 0], out_recv.at[p])


def per_device(tokens, norm_gain, norm_bias, keep_mask, projection, head_gain, traj_starts):
    any_spec = pl.BlockSpec(memory_space=pl.ANY)
    dma = pltpu.SemaphoreType.DMA
    return pl.pallas_call(
        kernel,
        out_shape=jax.ShapeDtypeStruct((2048, 256), BF16),
        in_specs=[any_spec] * 7,
        out_specs=any_spec,
        scratch_shapes=[
            pltpu.VMEM((1, D), F32),
            pltpu.VMEM((1, D), F32),
            pltpu.SMEM((8,), I32),
            pltpu.VMEM((OWN, D), BF16),
            pltpu.VMEM((OWN, D), I32),
            pltpu.VMEM((2, 2, OWN, D), BF16),
            pltpu.VMEM((2, 3, 4, 4, 128, 256), BF16),
            pltpu.VMEM((2, 3, 2, SPAN, 256), BF16),
            pltpu.VMEM((2, 2, SPAN, 256), F32),
            pltpu.VMEM((2, 2, 256, HEAD), BF16),
            pltpu.VMEM((2, 2, 4, 64, HEAD), BF16),
            pltpu.VMEM((2, 2, 4, 64, HEAD), BF16),
            pltpu.VMEM((2, 64, HEAD), F32),
            pltpu.VMEM((2, 16, 8, HEAD), F32),
            pltpu.VMEM((2, 16, 8, HEAD), F32),
            pltpu.VMEM((2, 2, 256, HEAD), BF16),
            pltpu.VMEM((2, 32, 8, HEAD), F32),
            pltpu.VMEM((2, 1, 256), F32),
            pltpu.VMEM((2, 2, SPAN, 256), BF16),
            dma((2, PARTS)),
            dma((4,)),
            dma((4, 3)),
            dma((2, 3, 2)),
            dma((len(UNITS), 4, 2)),
            dma((len(UNITS), 4, 2)),
            dma((2, PARTS)),
            dma((PARTS,)),
            dma((PARTS,)),
            dma((2, PARTS)),
            dma((3,)),
            dma((2,)),
            dma((2, 3)),
            dma((2, 4)),
            dma((2,)),
            dma((2,)),
            dma((2, 3)),
            dma((2, 4)),
            dma((2,)),
            dma((2,)),
            dma((2, 2)),
            dma((4,)),
        ],
        compiler_params=pltpu.CompilerParams(
            collective_id=0, has_side_effects=True, vmem_limit_bytes=63 * 1024 * 1024
        ),
    )(
        tokens, norm_gain.reshape(1, D), norm_bias.reshape(1, D), keep_mask, projection,
        head_gain.reshape(1, 256), traj_starts,
    )


def solution(mesh):
    placed = (
        P(("outer", "inner"), None),
        P(),
        P(),
        P(("outer", "inner"), None),
        P(None, "outer", "inner"),
        P("inner"),
        P(),
    )
    return jax.shard_map(
        per_device, mesh=mesh, in_specs=placed, out_specs=P("outer", "inner"), check_vma=False
    )
```

```python
import jax
import jax.numpy as jnp
from jax import lax
from jax.experimental import pallas as pl
from jax.experimental.pallas import tpu as pltpu
from jax.sharding import PartitionSpec as P

MESH = pl.DeviceIdType.MESH
F32, BF16, I32 = jnp.float32, jnp.bfloat16, jnp.int32
D, HEAD, SPAN = 2048, 128, 512
OWN = 256
DIRECT = 2
PARTS = 4
PART = OWN // PARTS
QUERY, KEY, VALUE = 0, 1, 2
UNITS = ((1, KEY), (0, KEY), (0, VALUE), (1, VALUE), (0, QUERY), (1, QUERY))


def core_of(dist):
    return ((dist + 1) // 2) % 2


def plane_at(head_plane, dist):
    up = (head_plane + dist) % 8
    down = (head_plane + 8 - dist) % 8
    return jnp.where(up % 2 == 0, up, down)


def kernel(
    tok_hbm, gain_hbm, bias_hbm, mask_hbm, proj_hbm, head_gain, traj_hbm, out,
    gain, bias, traj, tok, mask, x_all, w_all, qkv, inside, a_out, rz, local_c, t_all, tp, ps, local_in, prefix_in, gains, outs,
    in_sem, small_sem, wz_send, wz_recv, ring_send, ring_recv, tok_send, tok_recv, fwd_send, sib_recv, hg_send, hg_recv,
    rz_send, rz_recv, a2a_send, a2a_recv, local_send, local_recv, prefix_send, prefix_recv, out_send, out_recv,
):
    outer, z = lax.axis_index("outer"), lax.axis_index("inner")
    core, chip = outer % 2, outer // 2
    cx, cy = chip // 4, chip % 4
    pair, member = z // 2, z % 2
    along = jnp.where(core == 0, cx, cy)
    across = jnp.where(core == 0, cy, cx)

    def chip_at(a, b):
        return a * (4 - 3 * core) + b * (1 + 3 * core)

    a_next, a_prev = (along + 1) % 4, (along + 3) % 4
    b_next, b_prev = (across + 1) % 4, (across + 3) % 4

    def plane_dev(chip_id):
        return (chip_id * 2 + core, z)

    def column_dev(core_id, plane):
        return (chip * 2 + core_id, plane)

    dists = tuple(jnp.where((z + s) % 2 == 0, 2 * core, 3 - 2 * core) for s in range(2))
    own_slot = z % 2
    step = 2 * member - 1
    planes = tuple((z + step * d + 8) % 8 for d in dists)

    def remote(src, dst, send, recv, device):
        return pltpu.make_async_remote_copy(
            src_ref=src, dst_ref=dst, send_sem=send, recv_sem=recv, device_id=device, device_id_type=MESH
        )

    def wait_for(ref, sem):
        pltpu.make_async_copy(ref, ref, sem).wait()

    def in_copies(i):
        rows = pl.ds(i * PART, PART)
        return (
            pltpu.make_async_copy(tok_hbm.at[rows], tok.at[rows], in_sem.at[0, i]),
            pltpu.make_async_copy(mask_hbm.at[rows], mask.at[rows], in_sem.at[1, i]),
        )

    small_copies = (
        pltpu.make_async_copy(gain_hbm, gain, small_sem.at[0]),
        pltpu.make_async_copy(bias_hbm, bias, small_sem.at[1]),
        pltpu.make_async_copy(traj_hbm, traj, small_sem.at[2]),
    )
    for copy in in_copies(0) + small_copies:
        copy.start()
    for i in range(1, PARTS):
        for copy in in_copies(i):
            copy.start()

    barrier = pltpu.get_barrier_semaphore()

    def greet_plane(i, carry):
        pl.semaphore_signal(barrier, inc=1, device_id=plane_dev((chip + i) % 16), device_id_type=MESH)
        return carry

    def greet_column(i, carry):
        spot = (z * 2 + core + i) % 16
        pl.semaphore_signal(barrier, inc=1, device_id=column_dev(spot % 2, spot // 2), device_id_type=MESH)
        return carry

    lax.fori_loop(1, 16, greet_column, 0)
    lax.fori_loop(1, 16, greet_plane, 0)

    def wz_copy(d, w):
        src = proj_hbm.at[w]
        dst = w_all.at[own_slot, w, cx, cy, pl.ds(core * 64, 64)]
        return src, dst, wz_send.at[d, w], wz_recv.at[own_slot, w, core], column_dev(core_of(d), plane_at(z, d))

    def send_weights(w, which):
        for d in which:
            src, dst, send, recv, device = wz_copy(d, w)
            if d == 0:

                @pl.when(core == 0)
                def _():
                    pltpu.make_async_copy(src, dst, recv).start()

                @pl.when(core == 1)
                def _():
                    remote(src, dst, send, recv, device).start()

            else:
                remote(src, dst, send, recv, device).start()

    def send_gains():
        for d in (1, 2, 3):

            @pl.when(core == core_of(d))
            def _():
                remote(
                    head_gain, gains.at[own_slot], hg_send.at[d - 1], hg_recv.at[own_slot], column_dev(core, plane_at(z, d))
                ).start()

        @pl.when(core == 0)
        def _():
            pltpu.make_async_copy(head_gain, gains.at[own_slot], small_sem.at[3]).start()

    def wait_wz(u):
        s, w = UNITS[u]
        for half in range(2):
            wait_for(w_all.at[s, w, 0, 0, pl.ds(half * 64, 64)], wz_recv.at[s, w, half])

    def block(u, chip_id, rows=None):
        ref = w_all.at[(*UNITS[u], chip_id // 4, chip_id % 4)]
        return ref if rows is None else ref.at[pl.ds(rows, 64)]

    def line_x(u, b, rows=None):
        ref = w_all.at[(*UNITS[u], slice(None), b)]
        return ref if rows is None else ref.at[:, pl.ds(rows, 64)]

    def line_y(u, b, rows=None):
        ref = w_all.at[(*UNITS[u], b)]
        return ref if rows is None else ref.at[:, pl.ds(rows, 64)]

    def ring_sems(u, stage, way):
        return ring_send.at[u, stage, way], ring_recv.at[u, stage, way]

    a_devices = (plane_dev(chip_at(a_next, across)), plane_dev(chip_at(a_prev, across)))
    b_devices = (plane_dev(chip_at(along, b_next)), plane_dev(chip_at(along, b_prev)))

    def a1(u):
        wait_wz(u)
        for way in range(2):
            ref = block(u, chip)
            remote(ref, ref, *ring_sems(u, 0, way), a_devices[way]).start()

    def a_direct(u):
        wait_wz(u)
        ref = block(u, chip)
        remote(ref, ref, *ring_sems(u, 1, 0), plane_dev(chip_at((along + 2) % 4, across))).start()
        for way in range(2):
            remote(ref, ref, *ring_sems(u, 0, way), a_devices[way]).start()

    def wait_ring(u, stage):
        for way in range(2):
            ref = line_y(u, 0, 64 * way if stage == 3 else None) if stage >= 2 else block(u, 0, 64 * way if stage == 1 else None)
            wait_for(ref, ring_recv.at[u, stage, way])

    def a2(u):
        wait_ring(u, 0)
        for way in range(2):
            ref = block(u, chip_at(a_prev if way == 0 else a_next, across), 64 * way)
            remote(ref, ref, *ring_sems(u, 1, way), a_devices[way]).start()

    def b_send(u, stage, spots, halves):
        @pl.when(core == 0)
        def _():
            for way in range(2):
                ref = line_x(u, spots[way], 64 * way if halves else None)
                remote(ref, ref, *ring_sems(u, stage, way), b_devices[way]).start()

        @pl.when(core == 1)
        def _():
            for way in range(2):
                ref = line_y(u, spots[way], 64 * way if halves else None)
                remote(ref, ref, *ring_sems(u, stage, way), b_devices[way]).start()

    def b1(u):
        if u < DIRECT:
            wait_ring(u, 0)
            wait_for(block(u, 0), ring_recv.at[u, 1, 0])
        else:
            wait_ring(u, 1)
        b_send(u, 2, (across, across), False)

    def b2(u):
        wait_ring(u, 2)
        b_send(u, 3, (b_prev, b_next), True)

    def b_done(u):
        wait_ring(u, 3)

    def ring_wait_sends(u):
        for stage in range(4):
            if u < DIRECT and stage == 1:
                wait_for(block(u, 0), ring_send.at[u, 1, 0])
                continue
            for way in range(2):
                half = 64 * way if stage in (1, 3) else None
                ref = line_y(u, 0, half) if stage >= 2 else block(u, 0, half)
                wait_for(ref, ring_send.at[u, stage, way])

    partner = column_dev(core, z + 1 - 2 * member)
    sibling = column_dev(1 - core, z)

    def token_rows(c, m, i):
        return x_all.at[c, m, pl.ds(i * PART, PART)]

    def normalize(i):
        for copy in in_copies(i):
            copy.wait()

        def rows16(j, carry):
            rows = pl.ds(pl.multiple_of(i * PART + j * 16, 16), 16)
            values = tok[rows, :].astype(F32)
            center = values - jnp.mean(values, axis=-1, keepdims=True)
            spread = jnp.mean(center * center, axis=-1, keepdims=True)
            scaled = center * lax.rsqrt(spread + 1e-05) * gain[...] + bias[...]
            x_all[core, member, rows, :] = (scaled * (mask[rows, :].astype(F32) * (1.0 / 0.9))).astype(BF16)
            return carry

        lax.fori_loop(0, PART // 16, rows16, 0)

    def send_tokens(i):
        ref = token_rows(core, member, i)
        remote(ref, ref, tok_send.at[0, i], tok_recv.at[i], partner).start()
        remote(ref, ref, tok_send.at[1, i], sib_recv.at[0, i], sibling).start()

    def forward_tokens(i):
        ref = token_rows(core, 1 - member, i)
        wait_for(ref, tok_recv.at[i])
        remote(ref, ref, fwd_send.at[i], sib_recv.at[1, i], sibling).start()

    def project(s, w, m):
        weights = w_all.at[s, w]

        def rows256(c, carry):
            product = jnp.dot(x_all[c, m], weights[...].reshape(D, 256), preferred_element_type=F32)
            rows = pl.ds(pl.multiple_of(m * OWN, OWN), OWN)
            qkv[s, w, c, rows, :] = product.astype(BF16)
            return carry

        lax.fori_loop(0, 2, rows256, 0)

    def start_of(position):
        first = jnp.full_like(position, -1)
        for i in range(8):
            first = jnp.where(traj[i] <= position, traj[i], first)
        return first

    def keeps(first, length):
        return jnp.where(start_of(first + (length - 1)) < first, 1.0, 0.0).astype(F32)

    chip_first = chip * 8 * SPAN

    keep_spans = []

    def span_first(c):
        return chip_first + (c * 4 + pair) * SPAN

    def states(s):
        def one_span(c, carry):
            first = span_first(c)
            last_start = start_of(first + (SPAN - 1))
            spots = first + lax.broadcasted_iota(I32, (SPAN, HEAD), 0)
            kept = spots >= last_start
            for h in range(2):
                columns = slice(h * HEAD, (h + 1) * HEAD)
                values = jnp.where(kept, qkv[s, 2, c, :, columns].astype(F32), 0.0).astype(BF16)
                state = lax.dot_general(
                    qkv[s, 1, c, :, columns], values, (((0,), (0,)), ((), ())), preferred_element_type=F32
                )
                a_out[s, c, columns, :] = state.astype(BF16)
            return carry

        lax.fori_loop(0, 2, one_span, 0)

    def send_states(s):
        mine = dists[s]
        for i in range(1, 4):
            other = (mine + i) % 4
            remote(
                a_out.at[s, :, pl.ds(pl.multiple_of(other * 64, 64), 64)], rz.at[s, :, pair],
                rz_send.at[s, i - 1], rz_recv.at[s, pair],
                column_dev(core_of(other), plane_at(planes[s], other)),
            ).start()
        rz[s, :, pair] = a_out[s, :, pl.ds(pl.multiple_of(mine * 64, 64), 64), :]

    def wait_states(s):
        for i in range(1, 4):
            spot = (pair + i) % 4
            wait_for(rz.at[s, :, spot], rz_recv.at[s, spot])

    half = chip // 8
    eighth = chip % 8

    def chip_totals(s):
        total = jnp.zeros((64, HEAD), F32)
        for j in range(8):
            local_c[s, j // 4, j % 4] = total.astype(BF16)
            total = total * keep_spans[j] + rz[s, j // 4, j % 4].astype(F32)
        t_all[s] = total

        def send(i, carry):
            other = (chip + i) % 16
            remote(
                t_all.at[s, pl.ds(pl.multiple_of((other % 8) * 8, 8), 8)], tp.at[s, chip], a2a_send.at[s], a2a_recv.at[s],
                plane_dev(other),
            ).start()
            return carry

        lax.fori_loop(1, 16, send, 0)
        tp[s, chip] = t_all[s, pl.ds(pl.multiple_of(eighth * 8, 8), 8), :]

    def send_local(s):
        mine = dists[s]
        rows = pl.ds(pl.multiple_of(mine * 64, 64), 64)
        for i in range(1, 4):
            other = (mine + i) % 4
            plane = plane_at(planes[s], other)
            remote(
                local_c.at[s, :, plane // 2], local_in.at[s, :, rows],
                local_send.at[s, i - 1], local_recv.at[s, mine],
                column_dev(core_of(other), plane),
            ).start()
        local_in[s, :, rows, :] = local_c[s, :, pair]

    def prefixes(s):
        wait_for(tp.at[s, pl.ds(0, 15)], a2a_recv.at[s])
        total = jnp.zeros((8, HEAD), F32)
        for k in range(16):
            ps[s, k] = total
            if k < 15:
                total = total * keeps(k * 8 * SPAN, 8 * SPAN) + tp[s, k]
        mine = dists[s]
        spot = mine * 8 + eighth
        targets = []
        for near in range(4):
            dist = (mine + near) % 4
            targets.append((core_of(dist), plane_at(planes[s], dist), prefix_in.at[s, spot]))

        def to_chip(i, carry):
            other = half * 8 + (eighth + i) % 8
            for near, (core_id, plane, dst) in enumerate(targets):
                copy = remote(ps.at[s, other], dst, prefix_send.at[s], prefix_recv.at[s], (other * 2 + core_id, plane))
                if near == 0:
                    pl.when(i != 0)(copy.start)
                else:
                    copy.start()
            return carry

        lax.fori_loop(0, 8, to_chip, 0)
        prefix_in[s, spot] = ps[s, chip]

    def wait_prefix(s):
        wait_for(prefix_in.at[s, pl.ds(0, 31)], prefix_recv.at[s])

    def wait_local(s):
        for i in range(1, 4):
            spot = (dists[s] + i) % 4
            wait_for(local_in.at[s, :, pl.ds(0, 64)], local_recv.at[s, spot])

    def inside_terms(s):
        def one_span(c, carry):
            first = span_first(c)
            for top in (0, 256):
                span_keys = top + 256
                rows = first + top + lax.broadcasted_iota(I32, (256, 1), 0)
                spots = first + lax.broadcasted_iota(I32, (256, span_keys), 1)
                allowed = (spots <= rows) & (spots >= start_of(rows))
                for h in range(2):
                    columns = slice(h * HEAD, (h + 1) * HEAD)
                    scores = lax.dot_general(
                        qkv[s, 0, c, top:top + 256, columns], qkv[s, 1, c, :span_keys, columns],
                        (((1,), (1,)), ((), ())), preferred_element_type=F32,
                    )
                    rounded = jnp.where(allowed, scores, 0.0).astype(BF16)
                    inside[s, c, top:top + 256, columns] = jnp.dot(
                        rounded, qkv[s, 2, c, :span_keys, columns], preferred_element_type=F32
                    )
            return carry

        lax.fori_loop(0, 2, one_span, 0)

    def finish(s, c):
        first = span_first(c)
        reach = jnp.ones((), F32)
        for j in range(7):
            reach = jnp.where(j < c * 4 + pair, reach * keep_spans[j], reach)
        for top in (0, 256):
            rows = first + top + lax.broadcasted_iota(I32, (256, 1), 0)
            reached = start_of(rows) < first
            for h in range(2):
                columns = slice(h * HEAD, (h + 1) * HEAD)
                queries = qkv[s, 0, c, top:top + 256, columns]
                prefix = prefix_in[s, h * 16:(h + 1) * 16].reshape(HEAD, HEAD)
                state = local_in[s, c, columns, :].astype(F32) + prefix * reach
                high = state.astype(BF16)
                low = (state - high.astype(F32)).astype(BF16)
                term = jnp.dot(queries, high, preferred_element_type=F32)
                term += jnp.dot(queries, low, preferred_element_type=F32)
                mixed = inside[s, c, top:top + 256, columns] + jnp.where(reached, term, 0.0)
                scale_back = lax.rsqrt(jnp.mean(mixed * mixed, axis=-1, keepdims=True) + 1e-06)
                outs[s, c, top:top + 256, columns] = (mixed * scale_back * gains[s, :, columns]).astype(BF16)

    def send_out(s, c):
        rows = pl.ds(pl.multiple_of(pair * SPAN, SPAN), SPAN)
        device = column_dev(c, planes[s])
        args = (outs.at[s, c], out.at[rows])
        if c == 0:

            @pl.when(dists[s] == 0)
            def _():
                pltpu.make_async_copy(*args, out_recv.at[pair]).start()

            @pl.when(dists[s] != 0)
            def _():
                remote(*args, out_send.at[s, c], out_recv.at[pair], device).start()

        else:
            remote(*args, out_send.at[s, c], out_recv.at[pair], device).start()

    for copy in small_copies:
        copy.wait()
    normalize(0)
    pl.semaphore_wait(barrier, 30)
    send_tokens(0)
    send_weights(KEY, (0, 1, 2, 3))
    send_weights(VALUE, (0, 1, 2, 3))
    normalize(1)
    send_tokens(1)
    normalize(2)
    send_tokens(2)
    a_direct(0)
    normalize(3)
    send_tokens(3)
    a_direct(1)
    b1(0)
    a1(2)
    send_weights(QUERY, (3, 2, 1, 0))
    send_gains()
    forward_tokens(0)
    keep_spans.extend(keeps(chip_first + j * SPAN, SPAN) for j in range(8))
    a2(2)
    a1(3)
    b2(0)
    b1(1)
    forward_tokens(1)
    b1(2)
    a2(3)
    for i in range(PARTS):
        wait_for(token_rows(1 - core, member, i), sib_recv.at[0, i])
    b_done(0)
    project(1, KEY, member)
    b2(1)
    forward_tokens(2)
    b1(3)
    b2(2)
    b_done(1)
    project(0, KEY, member)
    forward_tokens(3)
    b_done(2)
    b2(3)
    a1(4)
    a1(5)
    project(0, VALUE, member)
    for i in range(PARTS):
        wait_for(token_rows(1 - core, 1 - member, i), sib_recv.at[1, i])
    project(0, KEY, 1 - member)
    project(0, VALUE, 1 - member)
    states(0)
    send_states(0)
    a2(4)
    a2(5)
    project(1, KEY, 1 - member)
    b1(4)
    b1(5)
    b_done(3)
    project(1, VALUE, member)
    project(1, VALUE, 1 - member)
    states(1)
    send_states(1)
    wait_states(0)
    chip_totals(0)
    send_local(0)
    b2(4)
    prefixes(0)
    wait_states(1)
    chip_totals(1)
    send_local(1)
    b2(5)
    b_done(4)
    for m in range(2):
        project(0, QUERY, m)
    inside_terms(0)
    prefixes(1)

    @pl.when(core == 0)
    def _():
        wait_for(gains.at[0], hg_recv.at[1 - own_slot])
        wait_for(gains.at[0], small_sem.at[3])

    @pl.when(core == 1)
    def _():
        for s in range(2):
            wait_for(gains.at[s], hg_recv.at[s])

    wait_local(0)
    wait_prefix(0)
    for c in range(2):
        finish(0, c)
        send_out(0, c)
    b_done(5)
    for m in range(2):
        project(1, QUERY, m)
    inside_terms(1)
    wait_local(1)
    wait_prefix(1)
    for c in range(2):
        finish(1, c)
        send_out(1, c)

    ref = w_all.at[0, 0, 0, 0, pl.ds(0, 64)]
    for w in range(3):
        for d in (1, 2, 3):
            wait_for(ref, wz_send.at[d, w])

    @pl.when(core == 1)
    def _():
        for w in range(3):
            wait_for(ref, wz_send.at[0, w])

    @pl.when(core == 0)
    def _():
        wait_for(gains.at[0], hg_send.at[2])

    @pl.when(core == 1)
    def _():
        for i in range(2):
            wait_for(gains.at[0], hg_send.at[i])

    for u in range(len(UNITS)):
        ring_wait_sends(u)
    for i in range(PARTS):
        ref = token_rows(0, 0, i)
        for sem in (tok_send.at[0, i], tok_send.at[1, i], fwd_send.at[i]):
            wait_for(ref, sem)
    for s in range(2):
        for i in range(3):
            wait_for(rz.at[s, :, 0], rz_send.at[s, i])
            wait_for(local_c.at[s, :, 0], local_send.at[s, i])
    for s in range(2):
        wait_for(tp.at[s, pl.ds(0, 15)], a2a_send.at[s])
        wait_for(prefix_in.at[s, pl.ds(0, 31)], prefix_send.at[s])
    for s in range(2):
        for c in range(2):
            if c == 0:

                @pl.when(dists[s] != 0)
                def _():
                    wait_for(outs.at[s, c], out_send.at[s, c])

            else:
                wait_for(outs.at[s, c], out_send.at[s, c])
    for p in range(4):
        wait_for(outs.at[0, 0], out_recv.at[p])


def per_device(tokens, norm_gain, norm_bias, keep_mask, projection, head_gain, traj_starts):
    any_spec = pl.BlockSpec(memory_space=pl.ANY)
    dma = pltpu.SemaphoreType.DMA
    return pl.pallas_call(
        kernel,
        out_shape=jax.ShapeDtypeStruct((2048, 256), BF16),
        in_specs=[any_spec] * 7,
        out_specs=any_spec,
        scratch_shapes=[
            pltpu.VMEM((1, D), F32),
            pltpu.VMEM((1, D), F32),
            pltpu.SMEM((8,), I32),
            pltpu.VMEM((OWN, D), BF16),
            pltpu.VMEM((OWN, D), I32),
            pltpu.VMEM((2, 2, OWN, D), BF16),
            pltpu.VMEM((2, 3, 4, 4, 128, 256), BF16),
            pltpu.VMEM((2, 3, 2, SPAN, 256), BF16),
            pltpu.VMEM((2, 2, SPAN, 256), F32),
            pltpu.VMEM((2, 2, 256, HEAD), BF16),
            pltpu.VMEM((2, 2, 4, 64, HEAD), BF16),
            pltpu.VMEM((2, 2, 4, 64, HEAD), BF16),
            pltpu.VMEM((2, 64, HEAD), F32),
            pltpu.VMEM((2, 16, 8, HEAD), F32),
            pltpu.VMEM((2, 16, 8, HEAD), F32),
            pltpu.VMEM((2, 2, 256, HEAD), BF16),
            pltpu.VMEM((2, 32, 8, HEAD), F32),
            pltpu.VMEM((2, 1, 256), F32),
            pltpu.VMEM((2, 2, SPAN, 256), BF16),
            dma((2, PARTS)),
            dma((4,)),
            dma((4, 3)),
            dma((2, 3, 2)),
            dma((len(UNITS), 4, 2)),
            dma((len(UNITS), 4, 2)),
            dma((2, PARTS)),
            dma((PARTS,)),
            dma((PARTS,)),
            dma((2, PARTS)),
            dma((3,)),
            dma((2,)),
            dma((2, 3)),
            dma((2, 4)),
            dma((2,)),
            dma((2,)),
            dma((2, 3)),
            dma((2, 4)),
            dma((2,)),
            dma((2,)),
            dma((2, 2)),
            dma((4,)),
        ],
        compiler_params=pltpu.CompilerParams(
            collective_id=0, has_side_effects=True, vmem_limit_bytes=63 * 1024 * 1024
        ),
    )(
        tokens, norm_gain.reshape(1, D), norm_bias.reshape(1, D), keep_mask, projection,
        head_gain.reshape(1, 256), traj_starts,
    )


def solution(mesh):
    placed = (
        P(("outer", "inner"), None),
        P(),
        P(),
        P(("outer", "inner"), None),
        P(None, "outer", "inner"),
        P("inner"),
        P(),
    )
    return jax.shard_map(
        per_device, mesh=mesh, in_specs=placed, out_specs=P("outer", "inner"), check_vma=False
    )
```
